512 devices in a mesh: gx: 32 (over y_hi, z, core), gy: 16 (over y_lo, x).
Axes of the slice: x: 4, y: 8 (y_hi: 2, y_lo: 4; y = y_hi * 4 + y_lo), z: 8, core: 2. Of those that a mesh axis runs over, the one named last changes fastest.
Arguments:
- positions: float32 [32, 16, 3, 128], P('gx', 'gy'), may hold values from 0 to 1
- species: int32 [32, 16, 128], P('gx', 'gy'), may hold values from 0 to 1
- neighbours: int32 [32, 16, 128, 8], P('gx', 'gy'), may hold values from 0 to 383, as said below
- counts: int32 [32, 16, 128], P('gx', 'gy'), may hold values from 1 to 8, as said below
- image_z: int32 [32, 16, 128, 8], P('gx', 'gy'), may hold values from -1 to 1
- send_lists: int32 [32, 16, 256], P('gx', 'gy'), may hold values from 0 to 127, as said below
- w_basis: float32 [8, 128], replicated, may hold values from -2 to 2
- w_center: float32 [2, 128], replicated, may hold values from -3 to 3
- w_neigh: float32 [2, 128], replicated, may hold values from -3 to 3
- w_env: float32 [128, 32], replicated, may hold values from -0.5 to 0.5
- w_latent: float32 [128, 128], replicated, may hold values from -0.5 to 0.5
- w_tensor: float32 [2, 32, 128], replicated, may hold values from -0.75 to 0.75
- w_out: float32 [128], replicated, may hold values from -0.5 to 0.5
Outputs:
- forces: float32 [32, 16, 3, 128], P('gx', 'gy')
- atom_energy: float32 [32, 16, 128], P('gx', 'gy')
The draws below stay inside these ranges and needn't reach their ends.
Inputs may be any that keep to these rules, and one draw needn't show every extreme that they name: `neighbours`: slots below 128 name another own atom of the box, never the atom itself; slots from 128 name ghost slots in the order of the ghost blocks. Padded slots hold indices of the same kind. `counts`: in every box some atom has all 8 slots live. `send_lists`: each of the four blocks (128, 64, 32, 32 entries) lists distinct atoms of the sending box.
All inputs are finite; a program needn't handle non-finite values.
Results may differ from the reference program's by a relative error of at most 0.00011.
Values sent between devices are 32-bit elements; how exact they have to be, the bound alone decides.
No kernel may reach another device: no remote copies, remote signals or barrier semaphores. Data moves between devices by JAX's collectives and lax.ppermute only.
A program may use at most 64 MiB of HBM per device.

```python
import jax
import jax.numpy as jnp
from jax import lax

A = 128
K = 8
EC = 128
TC = 32
NB = 8
BX = 32
BY = 16
GXF = 128
GYF = 64
GCN = 32
NGH = 256


def draw_neighbours(key, part):
    key = jax.random.fold_in(key, 11)
    key_own, key_ghost, key_pick = jax.random.split(key, 3)
    shape = (BX, BY, A, K)
    own_slot = (jnp.arange(A, dtype=jnp.int32)[:, None] + 1 + jax.random.randint(key_own, shape, 0, A - 1)) % A
    ghost_slot = A + jax.random.randint(key_ghost, shape, 0, NGH)
    picker = jax.random.randint(key_pick, shape, 0, 2)
    return jnp.where(picker == 0, own_slot, ghost_slot).astype(jnp.int32)


def draw_counts(key, part):
    key = jax.random.fold_in(key, 12)
    key_low, key_count, key_full = jax.random.split(key, 3)
    lowest = jax.random.randint(key_low, (BX, BY, 1), 1, K // 2 + 1)
    drawn = jax.random.randint(key_count, (BX, BY, A), lowest, K + 1)
    full_at = jax.random.randint(key_full, (BX, BY, 1), 0, A)
    return jnp.where(jnp.arange(A, dtype=jnp.int32)[None, None, :] == full_at, K, drawn).astype(jnp.int32)


def draw_send_lists(key, part):
    key = jax.random.fold_in(key, 13)
    key_list = jax.random.split(key, BX * BY * 4)
    orders = jax.vmap(lambda one_key: jax.random.permutation(one_key, A))(key_list).reshape(BX, BY, 4, A)
    return jnp.concatenate([orders[:, :, 0, :GXF], orders[:, :, 1, :GYF], orders[:, :, 2, :GCN], orders[:, :, 3, :GCN]], axis=2).astype(jnp.int32)


def touch_ends(result, key, smallest, high):
    extent = result.shape
    place = [jax.random.randint(jax.random.fold_in(key, axis), (), 0, extent[axis]) for axis in range(len(extent))]
    result = result.at[tuple(place)].set(smallest)
    longest = extent.index(max(extent))
    place[longest] = (place[longest] + 1) % extent[longest]
    return result.at[tuple(place)].set(high)


def shard_levels(own_key, dims, cuts, least, high):
    level, own = 1.0, jax.random.fold_in(own_key, 6)
    for position, shards_of in cuts:
        draws = jnp.exp(jax.random.uniform(jax.random.fold_in(own, position), (shards_of,), jnp.float32, least / len(cuts), high / len(cuts)))
        level = level * jnp.repeat(draws, dims[position] // shards_of).reshape([-1 if axis == position else 1 for axis in range(len(dims))])
    return level


def bell_draw(key, dims, scale, bound, kind=jnp.bfloat16):
    return jnp.clip(scale * jax.random.normal(key, dims, jnp.float32), -bound, bound).astype(kind)


def setup_inputs(seed: int = 0) -> dict:
    key_of = jax.random.split(jax.random.key(seed), 14)
    positions = jnp.clip(1.0 * jax.random.uniform(key_of[0], (BX, BY, 3, A), jnp.float32) ** shard_levels(key_of[0], (BX, BY, 3, A), ((0, 32), (1, 16)), -0.2, 0.2), 0.0, 1.0)
    species = touch_ends(jax.random.randint(key_of[1], (BX, BY, A), 0, 2), jax.random.fold_in(key_of[1], 1), 0, 1).astype(jnp.int32)
    neighbours = draw_neighbours(jax.random.fold_in(key_of[13], 71), 0)
    counts = draw_counts(jax.random.fold_in(key_of[13], 71), 0)
    image_z = touch_ends(jax.random.randint(key_of[4], (BX, BY, A, K), -1, 2), jax.random.fold_in(key_of[4], 1), -1, 1).astype(jnp.int32)
    send_lists = draw_send_lists(jax.random.fold_in(key_of[13], 71), 0)
    w_basis = bell_draw(key_of[6], (NB, EC), NB ** -0.5, 2.0, jnp.float32)
    w_center = bell_draw(key_of[7], (2, EC), 0.5, 3.0, jnp.float32)
    w_neigh = bell_draw(key_of[8], (2, EC), 0.5, 3.0, jnp.float32)
    w_env = bell_draw(key_of[9], (EC, TC), EC ** -0.5, 0.5, jnp.float32)
    w_latent = bell_draw(key_of[10], (EC, EC), EC ** -0.5, 0.5, jnp.float32)
    w_tensor = bell_draw(key_of[11], (2, TC, EC), (2 * TC) ** -0.5, 0.75, jnp.float32)
    w_out = bell_draw(key_of[12], (EC,), EC ** -0.5, 0.5, jnp.float32)
    return {"positions": positions, "species": species, "neighbours": neighbours, "counts": counts, "image_z": image_z, "send_lists": send_lists, "w_basis": w_basis, "w_center": w_center, "w_neigh": w_neigh, "w_env": w_env, "w_latent": w_latent, "w_tensor": w_tensor, "w_out": w_out}


PRECISE = lax.Precision.HIGHEST
SOFTEN = 0.25
ENV_SCALE = 0.25

def product(left, right):
    return jnp.dot(left, right, precision=PRECISE, preferred_element_type=jnp.float32)

def first_layer(pos_table, spec_table, neigh_idx, live_mask, image_lift, w_basis, w_center, w_neigh, w_env):
    atom_count, slot_count = neigh_idx.shape
    flat_idx = neigh_idx.reshape(-1)
    centre = jnp.broadcast_to(pos_table[:atom_count][:, None, :], (atom_count, slot_count, 3)).reshape(-1, 3)
    lift_z = image_lift.reshape(-1).astype(jnp.float32)
    zero_col = jnp.zeros_like(lift_z)
    displace = pos_table[flat_idx] - centre + jnp.stack([zero_col, zero_col, lift_z], axis=1)
    radius_sq = lax.optimization_barrier(jnp.sum(displace * displace, axis=1)) + SOFTEN
    radius = jnp.sqrt(radius_sq)
    unit_vec = displace / radius[:, None]
    envelope = live_mask * jnp.exp(-0.25 * radius_sq)
    nbasis = w_basis.shape[0]
    centres = 0.5 + 2.5 * jnp.arange(nbasis).astype(jnp.float32) / (nbasis - 1)
    basis_val = jnp.exp(-jnp.square((radius[:, None] - centres[None, :]) / 0.5))
    spec_c = jnp.broadcast_to(spec_table[:atom_count][:, None], (atom_count, slot_count)).reshape(-1)
    spec_n = spec_table[flat_idx]
    pre_act = product(basis_val, w_basis) + w_center[0] + spec_c[:, None] * (w_center[1] - w_center[0])
    pre_act = pre_act + w_neigh[0] + spec_n[:, None] * (w_neigh[1] - w_neigh[0])
    latent = jax.nn.silu(pre_act)
    weight_env = product(latent, w_env) * envelope[:, None]
    to_centre = jnp.concatenate([weight_env] + [weight_env * unit_vec[:, comp:comp + 1] for comp in range(3)], axis=1)
    to_neigh = jnp.concatenate([weight_env] + [-weight_env * unit_vec[:, comp:comp + 1] for comp in range(3)], axis=1)
    own_part = to_centre.reshape(atom_count, slot_count, -1).sum(axis=1)
    env_part = jax.ops.segment_sum(to_neigh, flat_idx, num_segments=pos_table.shape[0])
    env_part = env_part.at[:atom_count].add(own_part)
    return (ENV_SCALE * env_part, latent, unit_vec, envelope)

def second_layer(latent, unit_vec, envelope, env_all, neigh_idx, w_latent, w_tensor, w_out):
    atom_count, slot_count = neigh_idx.shape
    flat_idx = neigh_idx.reshape(-1)
    env_width = env_all.shape[1]
    channels = env_width // 4
    env_c = jnp.broadcast_to(env_all[:atom_count][:, None, :], (atom_count, slot_count, env_width)).reshape(-1, env_width)
    env_n = env_all[flat_idx]
    proj_c = env_c[:, :channels]
    proj_n = env_n[:, :channels]
    for comp in range(3):
        lower = (comp + 1) * channels
        proj_c = proj_c + env_c[:, lower:lower + channels] * unit_vec[:, comp:comp + 1]
        proj_n = proj_n - env_n[:, lower:lower + channels] * unit_vec[:, comp:comp + 1]
    hidden = jax.nn.silu(product(latent, w_latent) + product(proj_c, w_tensor[0]) + product(proj_n, w_tensor[1]))
    return envelope * product(latent + hidden, w_out)

def energy_split(edge_energy, neigh_idx, total_slots):
    atom_count, slot_count = neigh_idx.shape
    half_edge = 0.5 * edge_energy
    shares = jax.ops.segment_sum(half_edge, neigh_idx.reshape(-1), num_segments=total_slots)
    return shares.at[:atom_count].add(half_edge.reshape(atom_count, slot_count).sum(axis=1))

def pick_rows(table, send_lists):
    return jax.vmap(jax.vmap(lambda rows, index: rows[index]))(table, send_lists)

def to_ghosts(packet):
    cut_one = GXF
    cut_two = GXF + GYF
    cut_three = cut_two + GCN
    return jnp.concatenate([jnp.roll(packet[:, :, :cut_one], -1, axis=0), jnp.roll(packet[:, :, cut_one:cut_two], -1, axis=1), jnp.roll(packet[:, :, cut_two:cut_three], (-1, -1), axis=(0, 1)), jnp.roll(packet[:, :, cut_three:], (-1, 1), axis=(0, 1))], axis=2)

def to_owners(ghost, send_lists):
    cut_one = GXF
    cut_two = GXF + GYF
    cut_three = cut_two + GCN
    arrived = jnp.concatenate([jnp.roll(ghost[:, :, :cut_one], 1, axis=0), jnp.roll(ghost[:, :, cut_one:cut_two], 1, axis=1), jnp.roll(ghost[:, :, cut_two:cut_three], (1, 1), axis=(0, 1)), jnp.roll(ghost[:, :, cut_three:], (1, -1), axis=(0, 1))], axis=2)
    return jax.vmap(jax.vmap(lambda index, values: jnp.zeros((A, values.shape[1]), values.dtype).at[index].add(values)))(send_lists, arrived)

def ghost_offsets():
    rows = [(GXF, (1.0, 0.0, 0.0)), (GYF, (0.0, 1.0, 0.0)), (GCN, (1.0, 1.0, 0.0)), (GCN, (1.0, -1.0, 0.0))]
    return jnp.concatenate([jnp.broadcast_to(jnp.array(shift_vec, jnp.float32)[None, :], (length, 3)) for length, shift_vec in rows], axis=0)

def reference(positions, species, neighbours, counts, image_z, send_lists, w_basis, w_center, w_neigh, w_env, w_latent, w_tensor, w_out):
    boxes = BX * BY
    pos_rows = jnp.swapaxes(positions, 2, 3)
    spec_rows = species.astype(jnp.float32)
    own_table = jnp.concatenate([pos_rows, spec_rows[..., None]], axis=3)
    ghost_table = to_ghosts(pick_rows(own_table, send_lists))
    table_pos = jnp.concatenate([pos_rows, ghost_table[..., :3] + ghost_offsets()], axis=2)
    table_species = jnp.concatenate([spec_rows, ghost_table[..., 3]], axis=2)
    live_mask = (jnp.arange(K)[None, None, None, :] < counts[..., None]).astype(jnp.float32).reshape(BX, BY, A * K)

    def fold(values):
        return values.reshape((boxes,) + values.shape[2:])

    def unfold(values):
        return values.reshape((BX, BY) + values.shape[1:])
    common = (fold(table_pos), fold(table_species), fold(neighbours), fold(live_mask), fold(image_z))

    def layer_one(item):
        return first_layer(item[0], item[1], item[2], item[3], item[4], w_basis, w_center, w_neigh, w_env)

    def second_of(item, env_all):

        def energy_fn(latent, unit_vec, envelope, env_in):
            return second_layer(latent, unit_vec, envelope, env_in, item[2], w_latent, w_tensor, w_out)
        return energy_fn

    def phase_one(item):
        return layer_one(item)[0]
    env_part = unfold(lax.map(phase_one, common, batch_size=8))
    env_own = env_part[:, :, :A] + to_owners(env_part[:, :, A:], send_lists)
    env_all = jnp.concatenate([env_own, to_ghosts(pick_rows(env_own, send_lists))], axis=2)

    def phase_two(item):
        env_box = item[5]
        env_out, latent, unit_vec, envelope = layer_one(item)
        edge_energy, pull_back = jax.vjp(second_of(item, env_box), latent, unit_vec, envelope, env_box)
        grads = pull_back(jnp.ones_like(edge_energy))
        return (grads[3], energy_split(edge_energy, item[2], A + NGH))
    grad_env, energy_part = lax.map(phase_two, common + (fold(env_all),), batch_size=8)
    grad_env = unfold(grad_env)
    energy_part = unfold(energy_part)
    grad_own = grad_env[:, :, :A] + to_owners(grad_env[:, :, A:], send_lists)
    grad_all = jnp.concatenate([grad_own, to_ghosts(pick_rows(grad_own, send_lists))], axis=2)

    def phase_three(item):
        env_box = item[5]
        grad_box = item[6]

        def layer_pos(pos_table):
            return first_layer(pos_table, item[1], item[2], item[3], item[4], w_basis, w_center, w_neigh, w_env)
        outputs, pull_first = jax.vjp(layer_pos, item[0])
        edge_energy, pull_second = jax.vjp(second_of(item, env_box), outputs[1], outputs[2], outputs[3], env_box)
        grads = pull_second(jnp.ones_like(edge_energy))
        return pull_first((grad_box, grads[0], grads[1], grads[2]))[0]
    grad_pos = unfold(lax.map(phase_three, common + (fold(env_all), fold(grad_all)), batch_size=8))
    forces = -(grad_pos[:, :, :A] + to_owners(grad_pos[:, :, A:], send_lists))
    atom_energy = energy_part[:, :, :A] + to_owners(energy_part[:, :, A:, None], send_lists)[..., 0]
    return (jnp.swapaxes(forces, 2, 3), atom_energy)
```

```python
import jax
import jax.numpy as jnp
from jax import lax
from jax.experimental import pallas as pl
from jax.experimental.pallas import tpu as pltpu
from jax.sharding import PartitionSpec as P

F32 = jnp.float32
BF16 = jnp.bfloat16
ATOMS = 128
SLOTS = 8
EDGES = ATOMS * SLOTS
WIDE = 256
LONE = 128
TC = 32
VMEM_LIMIT = 48 * 1024 * 1024


def halves(x):
    high = x.astype(BF16)
    return high, (x - high.astype(F32)).astype(BF16)


def dot_nn(a, b):
    return lax.dot_general(a, b, (((1,), (0,)), ((), ())), preferred_element_type=F32)


def dot_nt(a, b):
    return lax.dot_general(a, b, (((1,), (1,)), ((), ())), preferred_element_type=F32)


def product(left, right):
    a, b = halves(left)
    c, d = halves(right)
    return dot_nn(a, c) + (dot_nn(a, d) + dot_nn(b, c))


def one_hot(index_row, rows):
    lines = lax.broadcasted_iota(jnp.int32, (rows, index_row.shape[1]), 0)
    return jnp.where(lines == index_row, 1.0, 0.0).astype(BF16)


def gather(high, low, hot):
    return dot_nn(high, hot) + dot_nn(low, hot)


def scatter(values, hot):
    high, low = halves(values)
    return dot_nt(high, hot) + dot_nt(low, hot)


def lanes(table, index):
    return jnp.take_along_axis(table, index, axis=1, mode="promise_in_bounds")


def spread(row):
    return jnp.broadcast_to(row, (8, row.shape[1]))


def sigmoid_parts(pre):
    gate = 1.0 / (1.0 + jnp.exp(-pre))
    value = pre * gate
    return value, gate + value * (1.0 - gate)


def four(weight, unit, sign):
    parts = [weight]
    for comp in range(3):
        parts.append((sign * weight) * unit[comp])
    return jnp.concatenate(parts, axis=0)


def basis_of(radius):
    step = lax.broadcasted_iota(jnp.int32, (8, radius.shape[1]), 0).astype(F32)
    gap = radius - (0.5 + 2.5 * step / 7.0)
    return jnp.exp(-4.0 * gap * gap), gap


def unit_rows(geo):
    return [geo[0:1], geo[1:2], geo[2:3]]


def geometry(dx, dy, dz, live):
    radius_sq = dx * dx + dy * dy + dz * dz + 0.25
    radius = jnp.sqrt(radius_sq)
    inverse = 1.0 / radius
    envelope = live * jnp.exp(-0.25 * radius_sq)
    return dx * inverse, dy * inverse, dz * inverse, envelope, radius


def first_kernel(
    own_ref, x_ref, yc_ref, wfeat_ref, wenv_ref, xc_ref, oy_ref, lat_ref, dlat_ref, wl_ref, geo_ref, count_ref, rank_ref
):
    sub = lax.broadcasted_iota(jnp.int32, (SLOTS, ATOMS), 0)
    lane = lax.broadcasted_iota(jnp.int32, (SLOTS, ATOMS), 1)
    x_send = x_ref[5:6]
    list_low = spread(x_ref[4:5])
    list_high = jnp.where(lane < 64, spread(yc_ref[5:6]), jnp.where(lane < 96, spread(yc_ref[29:30]), spread(x_send)))

    neigh = own_ref[8:16].astype(jnp.int32)
    live = sub < spread(own_ref[6:7]).astype(jnp.int32)
    ghost = neigh - ATOMS
    low = lanes(list_low, jnp.clip(ghost, 0, ATOMS - 1)).astype(jnp.int32)
    high = lanes(list_high, jnp.clip(ghost - ATOMS, 0, ATOMS - 1)).astype(jnp.int32)
    atom = jnp.where(ghost < 0, neigh, jnp.where(ghost < ATOMS, low, high))
    in_x = (ghost >= 0) & (ghost < 128)
    in_y = (ghost >= 128) & (ghost < 192)
    in_c = ghost >= 192
    live = live & (ghost < 224)

    def pick(line):
        values = lanes(spread(own_ref[line : line + 1]), atom)
        values = jnp.where(in_x, lanes(spread(x_ref[line : line + 1]), atom), values)
        values = jnp.where(in_y, lanes(spread(yc_ref[line : line + 1]), atom), values)
        return jnp.where(in_c, lanes(spread(yc_ref[24 + line : 25 + line]), atom), values)

    shift_x = jnp.where(in_x | in_c, 1.0, 0.0)
    shift_y = jnp.where(in_y | in_c, 1.0, 0.0)
    dx = pick(0) + shift_x - own_ref[0:1]
    dy = pick(1) + shift_y - own_ref[1:2]
    dz = pick(2) - own_ref[2:3] + own_ref[16:24]
    rows = list(geometry(dx, dy, dz, jnp.where(live, 1.0, 0.0)))
    rows.append(spread(own_ref[3:4]))
    rows.append(pick(3))
    box = jnp.where(in_x, 128, 0) + jnp.where(in_y, 256, 0) + jnp.where(in_c, 384, 0)
    rows.append((box + atom).astype(F32))
    for line, values in enumerate(rows):
        for k in range(SLOTS):
            geo_ref[line : line + 1, k * ATOMS : (k + 1) * ATOMS] = values[k : k + 1]
    geo_ref[8:16, 0:EDGES] = jnp.zeros((8, EDGES), F32)

    y_neigh = yc_ref[8:16].astype(jnp.int32)
    wanted = (sub < spread(yc_ref[6:7]).astype(jnp.int32)) & (y_neigh >= 352)
    wanted_f = jnp.where(wanted, 1.0, 0.0)
    y_atom = lanes(spread(x_send), jnp.clip(y_neigh - 256, 0, ATOMS - 1))
    before = jnp.where(
        lax.broadcasted_iota(jnp.int32, (ATOMS, ATOMS), 0) <= lax.broadcasted_iota(jnp.int32, (ATOMS, ATOMS), 1), 1.0, 0.0
    ).astype(BF16)
    upto = dot_nn(wanted_f.astype(BF16), before)
    totals = jnp.sum(wanted_f, axis=1, keepdims=True)
    running = jnp.zeros((1, 1), F32)
    starts = []
    for k in range(SLOTS):
        starts.append(running)
        running = running + totals[k : k + 1]
    rank = jnp.where(wanted, upto - 1.0 + jnp.concatenate(starts, axis=0), -1.0)
    rank_ref[0:8] = rank
    rank_ref[8:16] = y_atom
    count = jnp.sum(wanted_f).astype(jnp.int32)
    count_ref[0] = count
    blocks = (count + (LONE - 1)) // LONE

    def compact(block, carry):
        base = (block * LONE).astype(F32)
        line = lax.broadcasted_iota(jnp.int32, (LONE, ATOMS), 0).astype(F32) + base
        packed = jnp.zeros((8, LONE), F32)
        for k in range(SLOTS):
            hot = jnp.where(line == rank_ref[k : k + 1], 1.0, 0.0).astype(BF16)
            feats = jnp.where(sub == 0, lane.astype(F32), 0.0)
            feats = jnp.where(sub == 1, rank_ref[8 + k : 9 + k], feats)
            feats = jnp.where(sub == 2, yc_ref[16 + k : 17 + k], feats)
            feats = jnp.where(sub == 3, 1.0, feats)
            packed = packed + dot_nt(feats.astype(BF16), hot)
        centre = lanes(yc_ref[0:8], spread(packed[0:1]).astype(jnp.int32))
        other = lanes(x_ref[0:8], spread(packed[1:2]).astype(jnp.int32))
        ex = other[0:1] + 1.0 - centre[0:1]
        ey = other[1:2] - 1.0 - centre[1:2]
        ez = other[2:3] - centre[2:3] + packed[2:3]
        found = list(geometry(ex, ey, ez, packed[3:4])) + [centre[3:4], other[3:4], packed[1:2], packed[0:1]]
        spot = pl.ds(pl.multiple_of(EDGES + block * LONE, LONE), LONE)
        for number, values in enumerate(found):
            geo_ref[number : number + 1, spot] = values
        return carry

    lax.fori_loop(0, blocks, compact, 0)

    wfeat = wfeat_ref[...]
    wenv = wenv_ref[...]
    xc_ref[...] = jnp.zeros_like(xc_ref)
    oy_ref[...] = jnp.zeros_like(oy_ref)

    def edge_block(spot):
        geo = geo_ref[:, spot]
        basis, _ = basis_of(geo[4:5])
        line = lax.broadcasted_iota(jnp.int32, basis.shape, 0)
        extra = jnp.where(line == 0, 1.0, jnp.where(line == 1, geo[5:6], jnp.where(line == 2, geo[6:7], 0.0)))
        pre = product(wfeat, jnp.concatenate([basis, extra], axis=0))
        latent, slope = sigmoid_parts(pre)
        lat_ref[:, spot] = latent
        dlat_ref[:, spot] = slope
        plain = product(wenv, latent)
        wl_ref[:, spot] = plain
        weight = plain * (0.25 * geo[3:4])
        unit = unit_rows(geo)
        return geo, four(weight, unit, 1.0), four(weight, unit, -1.0)

    def main(block, carry):
        spot = pl.ds(pl.multiple_of(block * WIDE, WIDE), WIDE)
        geo, centre, other = edge_block(spot)
        sums = scatter(other, one_hot(geo[7:8].astype(jnp.int32), 512))
        oy_ref[0:128] += sums[:, 0:128] + (centre[:, 0:128] + centre[:, 128:256])
        xc_ref[0:128] += sums[:, 128:256]
        oy_ref[128:256] += sums[:, 256:384]
        xc_ref[128:256] += sums[:, 384:512]
        return carry

    lax.fori_loop(0, EDGES // WIDE, main, 0)

    def lone(block, carry):
        spot = pl.ds(pl.multiple_of(EDGES + block * LONE, LONE), LONE)
        geo, centre, other = edge_block(spot)
        xc_ref[0:128] += scatter(other, one_hot(geo[7:8].astype(jnp.int32), 128))
        oy_ref[128:256] += scatter(centre, one_hot(geo[8:9].astype(jnp.int32), 128))
        return carry

    lax.fori_loop(0, blocks, lone, 0)


def fill_tables(up_ref, down_ref, from_below_ref, from_above_ref, table_ref):
    own = down_ref[0:128] + from_below_ref[0:128]
    in_x = down_ref[128:256] + from_below_ref[128:256]
    in_y = up_ref[0:128] + from_above_ref[0:128]
    in_c = up_ref[128:256] + from_above_ref[128:256]
    for place, values in enumerate((own, in_x, in_y, in_c)):
        high, low = halves(values)
        table_ref[0:128, place * 128 : (place + 1) * 128] = high
        table_ref[128:256, place * 128 : (place + 1) * 128] = low
    return own


def fetch(table_ref, spot, hot):
    both = dot_nn(table_ref[:, spot], hot)
    return both[0:128] + both[128:256]


def project(rows, unit, sign):
    total = rows[0:TC]
    for comp in range(3):
        total = total + (sign * unit[comp]) * rows[(comp + 1) * TC : (comp + 2) * TC]
    return total


def second_kernel(
    count_ref, up_ref, down_ref, below_ref, above_ref, lat_ref, geo_ref, wlat_t_ref, wlat_ref, wten_t_ref, wten_ref, wout_ref,
    xc_ref, oy_ref, glat_ref, rows_ref, table_ref,
):
    own = fill_tables(up_ref, down_ref, below_ref, above_ref, table_ref)
    blocks = (count_ref[0] + (LONE - 1)) // LONE
    wout = wout_ref[...]
    xc_ref[...] = jnp.zeros_like(xc_ref)
    oy_ref[...] = jnp.zeros_like(oy_ref)

    def edge_block(spot, geo, env_c, env_n):
        unit = unit_rows(geo)
        envelope = geo[3:4]
        latent = lat_ref[:, spot]
        both = jnp.concatenate([project(env_c, unit, 1.0), project(env_n, unit, -1.0)], axis=0)
        pre = product(wlat_t_ref[...], latent) + product(wten_t_ref[...], both)
        hidden, slope = sigmoid_parts(pre)
        read = jnp.sum(wout * (latent + hidden), axis=0, keepdims=True)
        direct = wout * envelope
        grad_pre = direct * slope
        glat_ref[:, spot] = direct + product(wlat_ref[...], grad_pre)
        grad_both = product(wten_ref[...], grad_pre)
        grad_c, grad_n = grad_both[0:TC], grad_both[TC : 2 * TC]
        found = [read, 0.5 * envelope * read]
        for comp in range(3):
            lines = slice((comp + 1) * TC, (comp + 2) * TC)
            found.append(jnp.sum(env_c[lines] * grad_c - env_n[lines] * grad_n, axis=0, keepdims=True))
        for number, values in enumerate(found):
            rows_ref[number : number + 1, spot] = values
        return four(grad_c, unit, 1.0), four(grad_n, unit, -1.0)

    def main(block, carry):
        spot = pl.ds(pl.multiple_of(block * WIDE, WIDE), WIDE)
        geo = geo_ref[:, spot]
        hot = one_hot(geo[7:8].astype(jnp.int32), 512)
        env_n = fetch(table_ref, slice(0, 512), hot)
        centre, other = edge_block(spot, geo, jnp.concatenate([own, own], axis=1), env_n)
        sums = scatter(other, hot)
        oy_ref[0:128] += sums[:, 0:128] + (centre[:, 0:128] + centre[:, 128:256])
        xc_ref[0:128] += sums[:, 128:256]
        oy_ref[128:256] += sums[:, 256:384]
        xc_ref[128:256] += sums[:, 384:512]
        return carry

    lax.fori_loop(0, EDGES // WIDE, main, 0)

    def lone(block, carry):
        spot = pl.ds(pl.multiple_of(EDGES + block * LONE, LONE), LONE)
        geo = geo_ref[:, spot]
        hot_n = one_hot(geo[7:8].astype(jnp.int32), 128)
        hot_c = one_hot(geo[8:9].astype(jnp.int32), 128)
        env_n = fetch(table_ref, slice(128, 256), hot_n)
        env_c = fetch(table_ref, slice(256, 384), hot_c)
        centre, other = edge_block(spot, geo, env_c, env_n)
        xc_ref[0:128] += scatter(other, hot_n)
        oy_ref[128:256] += scatter(centre, hot_c)
        return carry

    lax.fori_loop(0, blocks, lone, 0)


def third_kernel(
    count_ref, up_ref, down_ref, below_ref, above_ref, dlat_ref, wl_ref, glat_ref, geo_ref, rows_ref, wenv_ref, wbasis_ref,
    yc_ref, ox_ref, table_ref,
):
    own = fill_tables(up_ref, down_ref, below_ref, above_ref, table_ref)
    blocks = (count_ref[0] + (LONE - 1)) // LONE
    yc_ref[...] = jnp.zeros_like(yc_ref)
    ox_ref[...] = jnp.zeros_like(ox_ref)

    def edge_block(spot, geo, grad_c, grad_n):
        unit = unit_rows(geo)
        envelope, radius = geo[3:4], geo[4:5]
        rows = rows_ref[:, spot]
        plain = wl_ref[:, spot]
        grad_w = 0.25 * (project(grad_c, unit, 1.0) + project(grad_n, unit, -1.0))
        weight = plain * (0.25 * envelope)
        grad_env = rows[0:1] + jnp.sum(grad_w * plain, axis=0, keepdims=True)
        grad_lat = glat_ref[:, spot] + product(wenv_ref[...], grad_w * envelope)
        grad_pre = grad_lat * dlat_ref[:, spot]
        grad_basis = product(wbasis_ref[...], grad_pre)
        basis, gap = basis_of(radius)
        grad_r = jnp.sum(grad_basis * (-8.0 * gap * basis), axis=0, keepdims=True)
        inverse = 1.0 / radius
        along = []
        for comp in range(3):
            lines = slice((comp + 1) * TC, (comp + 2) * TC)
            along.append(rows[2 + comp : 3 + comp] + jnp.sum(weight * (grad_c[lines] - grad_n[lines]), axis=0, keepdims=True))
            grad_r = grad_r - along[comp] * unit[comp] * inverse
        grad_sq = grad_r * (0.5 * inverse) - 0.25 * envelope * grad_env
        force = [-(along[comp] * inverse + 2.0 * radius * unit[comp] * grad_sq) for comp in range(3)]
        line = lax.broadcasted_iota(jnp.int32, (8, envelope.shape[1]), 0)
        packed = jnp.where(line == 3, rows[1:2], 0.0)
        for comp in range(3):
            packed = jnp.where(line == comp, force[comp], packed)
        return packed, jnp.where(line == 3, packed, -packed)

    def main(block, carry):
        spot = pl.ds(pl.multiple_of(block * WIDE, WIDE), WIDE)
        geo = geo_ref[:, spot]
        hot = one_hot(geo[7:8].astype(jnp.int32), 512)
        grad_n = fetch(table_ref, slice(0, 512), hot)
        other, centre = edge_block(spot, geo, jnp.concatenate([own, own], axis=1), grad_n)
        sums = scatter(other, hot)
        ox_ref[0:8] += sums[:, 0:128] + (centre[:, 0:128] + centre[:, 128:256])
        ox_ref[8:16] += sums[:, 128:256]
        yc_ref[0:8] += sums[:, 256:384]
        yc_ref[8:16] += sums[:, 384:512]
        return carry

    lax.fori_loop(0, EDGES // WIDE, main, 0)

    def lone(block, carry):
        spot = pl.ds(pl.multiple_of(EDGES + block * LONE, LONE), LONE)
        geo = geo_ref[:, spot]
        hot_n = one_hot(geo[7:8].astype(jnp.int32), 128)
        hot_c = one_hot(geo[8:9].astype(jnp.int32), 128)
        grad_n = fetch(table_ref, slice(128, 256), hot_n)
        grad_c = fetch(table_ref, slice(256, 384), hot_c)
        other, centre = edge_block(spot, geo, grad_c, grad_n)
        ox_ref[8:16] += scatter(other, hot_n)
        yc_ref[0:8] += scatter(centre, hot_c)
        return carry

    lax.fori_loop(0, blocks, lone, 0)


def call(kernel, out_shape, in_specs, out_specs, scratch, cost):
    return pl.pallas_call(
        kernel,
        out_shape=out_shape,
        in_specs=in_specs,
        out_specs=out_specs,
        scratch_shapes=scratch,
        compiler_params=pltpu.CompilerParams(vmem_limit_bytes=VMEM_LIMIT),
        cost_estimate=pl.CostEstimate(flops=cost, bytes_accessed=1 << 20, transcendentals=1 << 18),
    )


def shape(*dims):
    return jax.ShapeDtypeStruct(dims, F32)


IN_VMEM = pl.BlockSpec(memory_space=pltpu.VMEM)
IN_SMEM = pl.BlockSpec(memory_space=pltpu.SMEM)


def step(block, axis, distance):
    size = lax.axis_size(axis)
    return lax.ppermute(block, axis, [(i, (i + distance) % size) for i in range(size)])


def butterfly(xc, oy):
    from_left = step(xc, "gx", 1)
    from_right = step(oy, "gx", -1)
    here = oy + from_left
    beside = xc + from_right
    up = jnp.concatenate([here[128:256], beside[128:256]], axis=0)
    down = jnp.concatenate([here[0:128], beside[0:128]], axis=0)
    return up, down, step(up, "gy", 1), step(down, "gy", -1)


def local(
    positions, species, neighbours, counts, image_z, send_lists, w_basis, w_center, w_neigh, w_env, w_latent, w_tensor, w_out
):
    base = jnp.concatenate(
        [
            positions[0, 0],
            species[0].astype(F32),
            send_lists[0, 0].reshape(2, ATOMS).astype(F32),
            counts[0].astype(F32),
            jnp.zeros((1, ATOMS), F32),
        ],
        axis=0,
    )
    in_x = step(base, "gx", -1)
    own = jnp.concatenate([base, neighbours[0, 0].T.astype(F32), image_z[0, 0].T.astype(F32)], axis=0)
    in_yc = step(jnp.concatenate([own, in_x], axis=0), "gy", -1)

    wfeat = jnp.concatenate(
        [w_basis, (w_center[0] + w_neigh[0])[None], (w_center[1] - w_center[0])[None], (w_neigh[1] - w_neigh[0])[None],
         jnp.zeros((5, 128), F32)], axis=0
    ).T
    xc, oy, lat, dlat, wl, geo, count = call(
        first_kernel,
        (shape(256, 128), shape(256, 128), shape(128, 2 * EDGES), shape(128, 2 * EDGES), shape(32, 2 * EDGES),
         shape(16, 2 * EDGES), jax.ShapeDtypeStruct((1,), jnp.int32)),
        [IN_VMEM] * 5,
        (IN_VMEM,) * 6 + (IN_SMEM,),
        [pltpu.VMEM((16, ATOMS), F32)],
        500_000_000,
    )(own, in_x, in_yc, wfeat, w_env.T)
    up, down, below, above = butterfly(xc, oy)
    wten = w_tensor.reshape(2 * TC, 128)
    xc, oy, glat, rows = call(
        second_kernel,
        (shape(256, 128), shape(256, 128), shape(128, 2 * EDGES), shape(8, 2 * EDGES)),
        [IN_SMEM] + [IN_VMEM] * 11,
        (IN_VMEM,) * 4,
        [pltpu.VMEM((256, 512), BF16)],
        1_000_000_000,
    )(count, up, down, below, above, lat, geo, w_latent.T, w_latent, wten.T, wten, w_out[:, None])
    up, down, below, above = butterfly(xc, oy)
    yc, ox = call(
        third_kernel,
        (shape(16, 128), shape(16, 128)),
        [IN_SMEM] + [IN_VMEM] * 11,
        (IN_VMEM,) * 2,
        [pltpu.VMEM((256, 512), BF16)],
        500_000_000,
    )(count, up, down, below, above, dlat, wl, glat, geo, rows, w_env, w_basis)
    yc = step(yc, "gy", 1)
    ox = ox + yc
    total = ox[0:8] + step(ox[8:16], "gx", 1)
    return (total[0:3][None, None], total[3][None, None])


def solution(mesh):
    part = P("gx", "gy", None)
    wide = P("gx", "gy", None, None)
    return jax.shard_map(
        local,
        mesh=mesh,
        in_specs=(wide, part, wide, part, wide, part) + (P(),) * 7,
        out_specs=(wide, part),
        check_vma=False,
    )
```

```python
import jax
import jax.numpy as jnp
from jax import lax
from jax.experimental import pallas as pl
from jax.experimental.pallas import tpu as pltpu
from jax.sharding import PartitionSpec as P

F32 = jnp.float32
BF16 = jnp.bfloat16
ATOMS = 128
SLOTS = 8
EDGES = ATOMS * SLOTS
WIDE = 256
LONE = 128
TC = 32
VMEM_LIMIT = 48 * 1024 * 1024


def halves(x):
    high = x.astype(BF16)
    return high, (x - high.astype(F32)).astype(BF16)


def dot_nn(a, b):
    return lax.dot_general(a, b, (((1,), (0,)), ((), ())), preferred_element_type=F32)


def dot_nt(a, b):
    return lax.dot_general(a, b, (((1,), (1,)), ((), ())), preferred_element_type=F32)


def product(left, right):
    a, b = halves(left)
    c, d = halves(right)
    return dot_nn(a, c) + (dot_nn(a, d) + dot_nn(b, c))


def one_hot(index_row, rows):
    lines = lax.broadcasted_iota(jnp.int32, (rows, index_row.shape[1]), 0)
    return jnp.where(lines == index_row, 1.0, 0.0).astype(BF16)


def gather(high, low, hot):
    return dot_nn(high, hot) + dot_nn(low, hot)


def scatter(values, hot):
    high, low = halves(values)
    return dot_nt(high, hot) + dot_nt(low, hot)


def lanes(table, index):
    return jnp.take_along_axis(table, index, axis=1, mode="promise_in_bounds")


def spread(row):
    return jnp.broadcast_to(row, (8, row.shape[1]))


def sigmoid_parts(pre):
    gate = 1.0 / (1.0 + jnp.exp(-pre))
    value = pre * gate
    return value, gate + value * (1.0 - gate)


def four(weight, unit, sign):
    parts = [weight]
    for comp in range(3):
        parts.append((sign * weight) * unit[comp])
    return jnp.concatenate(parts, axis=0)


def basis_of(radius):
    step = lax.broadcasted_iota(jnp.int32, (8, radius.shape[1]), 0).astype(F32)
    gap = radius - (0.5 + 2.5 * step / 7.0)
    return jnp.exp(-4.0 * gap * gap), gap


def unit_rows(geo):
    return [geo[0:1], geo[1:2], geo[2:3]]


def geometry(dx, dy, dz, live):
    radius_sq = dx * dx + dy * dy + dz * dz + 0.25
    radius = jnp.sqrt(radius_sq)
    inverse = 1.0 / radius
    envelope = live * jnp.exp(-0.25 * radius_sq)
    return dx * inverse, dy * inverse, dz * inverse, envelope, radius


def first_kernel(
    own_ref, x_ref, yc_ref, wfeat_ref, wenv_ref, xc_ref, oy_ref, lat_ref, dlat_ref, wl_ref, geo_ref, count_ref, rank_ref
):
    sub = lax.broadcasted_iota(jnp.int32, (SLOTS, ATOMS), 0)
    lane = lax.broadcasted_iota(jnp.int32, (SLOTS, ATOMS), 1)
    x_send = x_ref[5:6]
    list_low = spread(x_ref[4:5])
    list_high = jnp.where(lane < 64, spread(yc_ref[5:6]), jnp.where(lane < 96, spread(yc_ref[29:30]), spread(x_send)))

    neigh = own_ref[8:16].astype(jnp.int32)
    live = sub < spread(own_ref[6:7]).astype(jnp.int32)
    ghost = neigh - ATOMS
    low = lanes(list_low, jnp.clip(ghost, 0, ATOMS - 1)).astype(jnp.int32)
    high = lanes(list_high, jnp.clip(ghost - ATOMS, 0, ATOMS - 1)).astype(jnp.int32)
    atom = jnp.where(ghost < 0, neigh, jnp.where(ghost < ATOMS, low, high))
    in_x = (ghost >= 0) & (ghost < 128)
    in_y = (ghost >= 128) & (ghost < 192)
    in_c = ghost >= 192
    live = live & (ghost < 224)

    def pick(line):
        values = lanes(spread(own_ref[line : line + 1]), atom)
        values = jnp.where(in_x, lanes(spread(x_ref[line : line + 1]), atom), values)
        values = jnp.where(in_y, lanes(spread(yc_ref[line : line + 1]), atom), values)
        return jnp.where(in_c, lanes(spread(yc_ref[24 + line : 25 + line]), atom), values)

    shift_x = jnp.where(in_x | in_c, 1.0, 0.0)
    shift_y = jnp.where(in_y | in_c, 1.0, 0.0)
    dx = pick(0) + shift_x - own_ref[0:1]
    dy = pick(1) + shift_y - own_ref[1:2]
    dz = pick(2) - own_ref[2:3] + own_ref[16:24]
    rows = list(geometry(dx, dy, dz, jnp.where(live, 1.0, 0.0)))
    rows.append(spread(own_ref[3:4]))
    rows.append(pick(3))
    box = jnp.where(in_x, 128, 0) + jnp.where(in_y, 256, 0) + jnp.where(in_c, 384, 0)
    rows.append((box + atom).astype(F32))
    for line, values in enumerate(rows):
        for k in range(SLOTS):
            geo_ref[line : line + 1, k * ATOMS : (k + 1) * ATOMS] = values[k : k + 1]
    geo_ref[8:16, 0:EDGES] = jnp.zeros((8, EDGES), F32)

    y_neigh = yc_ref[8:16].astype(jnp.int32)
    wanted = (sub < spread(yc_ref[6:7]).astype(jnp.int32)) & (y_neigh >= 352)
    wanted_f = jnp.where(wanted, 1.0, 0.0)
    y_atom = lanes(spread(x_send), jnp.clip(y_neigh - 256, 0, ATOMS - 1))
    before = jnp.where(
        lax.broadcasted_iota(jnp.int32, (ATOMS, ATOMS), 0) <= lax.broadcasted_iota(jnp.int32, (ATOMS, ATOMS), 1), 1.0, 0.0
    ).astype(BF16)
    upto = dot_nn(wanted_f.astype(BF16), before)
    totals = jnp.sum(wanted_f, axis=1, keepdims=True)
    running = jnp.zeros((1, 1), F32)
    starts = []
    for k in range(SLOTS):
        starts.append(running)
        running = running + totals[k : k + 1]
    rank = jnp.where(wanted, upto - 1.0 + jnp.concatenate(starts, axis=0), -1.0)
    rank_ref[0:8] = rank
    rank_ref[8:16] = y_atom
    count = jnp.sum(wanted_f).astype(jnp.int32)
    count_ref[0] = count
    blocks = (count + (LONE - 1)) // LONE

    def compact(block, carry):
        base = (block * LONE).astype(F32)
        line = lax.broadcasted_iota(jnp.int32, (LONE, ATOMS), 0).astype(F32) + base
        packed = jnp.zeros((8, LONE), F32)
        for k in range(SLOTS):
            hot = jnp.where(line == rank_ref[k : k + 1], 1.0, 0.0).astype(BF16)
            feats = jnp.where(sub == 0, lane.astype(F32), 0.0)
            feats = jnp.where(sub == 1, rank_ref[8 + k : 9 + k], feats)
            feats = jnp.where(sub == 2, yc_ref[16 + k : 17 + k], feats)
            feats = jnp.where(sub == 3, 1.0, feats)
            packed = packed + dot_nt(feats.astype(BF16), hot)
        centre = lanes(yc_ref[0:8], spread(packed[0:1]).astype(jnp.int32))
        other = lanes(x_ref[0:8], spread(packed[1:2]).astype(jnp.int32))
        ex = other[0:1] + 1.0 - centre[0:1]
        ey = other[1:2] - 1.0 - centre[1:2]
        ez = other[2:3] - centre[2:3] + packed[2:3]
        found = list(geometry(ex, ey, ez, packed[3:4])) + [centre[3:4], other[3:4], packed[1:2], packed[0:1]]
        spot = pl.ds(pl.multiple_of(EDGES + block * LONE, LONE), LONE)
        for number, values in enumerate(found):
            geo_ref[number : number + 1, spot] = values
        return carry

    lax.fori_loop(0, blocks, compact, 0)

    wfeat = wfeat_ref[...]
    wenv = wenv_ref[...]
    xc_ref[...] = jnp.zeros_like(xc_ref)
    oy_ref[...] = jnp.zeros_like(oy_ref)

    def edge_block(spot):
        geo = geo_ref[:, spot]
        basis, _ = basis_of(geo[4:5])
        line = lax.broadcasted_iota(jnp.int32, basis.shape, 0)
        extra = jnp.where(line == 0, 1.0, jnp.where(line == 1, geo[5:6], jnp.where(line == 2, geo[6:7], 0.0)))
        pre = product(wfeat, jnp.concatenate([basis, extra], axis=0))
        latent, slope = sigmoid_parts(pre)
        lat_ref[:, spot] = latent
        dlat_ref[:, spot] = slope
        plain = product(wenv, latent)
        wl_ref[:, spot] = plain
        weight = plain * (0.25 * geo[3:4])
        unit = unit_rows(geo)
        return geo, four(weight, unit, 1.0), four(weight, unit, -1.0)

    def main(block, carry):
        spot = pl.ds(pl.multiple_of(block * WIDE, WIDE), WIDE)
        geo, centre, other = edge_block(spot)
        sums = scatter(other, one_hot(geo[7:8].astype(jnp.int32), 512))
        oy_ref[0:128] += sums[:, 0:128] + (centre[:, 0:128] + centre[:, 128:256])
        xc_ref[0:128] += sums[:, 128:256]
        oy_ref[128:256] += sums[:, 256:384]
        xc_ref[128:256] += sums[:, 384:512]
        return carry

    lax.fori_loop(0, EDGES // WIDE, main, 0)

    def lone(block, carry):
        spot = pl.ds(pl.multiple_of(EDGES + block * LONE, LONE), LONE)
        geo, centre, other = edge_block(spot)
        xc_ref[0:128] += scatter(other, one_hot(geo[7:8].astype(jnp.int32), 128))
        oy_ref[128:256] += scatter(centre, one_hot(geo[8:9].astype(jnp.int32), 128))
        return carry

    lax.fori_loop(0, blocks, lone, 0)


def fill_tables(odd_ref, one_ref, two_ref, one_in_ref, two_in_ref, table_ref):
    odd = odd_ref[0] == 1
    one = one_ref[...] + one_in_ref[...]
    two = two_ref[...] + two_in_ref[...]
    down = jnp.where(odd, two, one)
    up = jnp.where(odd, one, two)
    own = down[0:128]
    for place, values in enumerate((own, down[128:256], up[0:128], up[128:256])):
        high, low = halves(values)
        table_ref[0:128, place * 128 : (place + 1) * 128] = high
        table_ref[128:256, place * 128 : (place + 1) * 128] = low
    return own


def fetch(table_ref, spot, hot):
    both = dot_nn(table_ref[:, spot], hot)
    return both[0:128] + both[128:256]


def project(rows, unit, sign):
    total = rows[0:TC]
    for comp in range(3):
        total = total + (sign * unit[comp]) * rows[(comp + 1) * TC : (comp + 2) * TC]
    return total


def second_kernel(
    count_ref, odd_ref, one_ref, two_ref, one_in_ref, two_in_ref, lat_ref, geo_ref, wlat_t_ref, wlat_ref, wten_t_ref, wten_ref, wout_ref,
    xc_ref, oy_ref, glat_ref, rows_ref, table_ref,
):
    own = fill_tables(odd_ref, one_ref, two_ref, one_in_ref, two_in_ref, table_ref)
    blocks = (count_ref[0] + (LONE - 1)) // LONE
    wout = wout_ref[...]
    xc_ref[...] = jnp.zeros_like(xc_ref)
    oy_ref[...] = jnp.zeros_like(oy_ref)

    def edge_block(spot, geo, env_c, env_n):
        unit = unit_rows(geo)
        envelope = geo[3:4]
        latent = lat_ref[:, spot]
        both = jnp.concatenate([project(env_c, unit, 1.0), project(env_n, unit, -1.0)], axis=0)
        pre = product(wlat_t_ref[...], latent) + product(wten_t_ref[...], both)
        hidden, slope = sigmoid_parts(pre)
        read = jnp.sum(wout * (latent + hidden), axis=0, keepdims=True)
        direct = wout * envelope
        grad_pre = direct * slope
        glat_ref[:, spot] = direct + product(wlat_ref[...], grad_pre)
        grad_both = product(wten_ref[...], grad_pre)
        grad_c, grad_n = grad_both[0:TC], grad_both[TC : 2 * TC]
        found = [read, 0.5 * envelope * read]
        for comp in range(3):
            lines = slice((comp + 1) * TC, (comp + 2) * TC)
            found.append(jnp.sum(env_c[lines] * grad_c - env_n[lines] * grad_n, axis=0, keepdims=True))
        for number, values in enumerate(found):
            rows_ref[number : number + 1, spot] = values
        return four(grad_c, unit, 1.0), four(grad_n, unit, -1.0)

    def main(block, carry):
        spot = pl.ds(pl.multiple_of(block * WIDE, WIDE), WIDE)
        geo = geo_ref[:, spot]
        hot = one_hot(geo[7:8].astype(jnp.int32), 512)
        env_n = fetch(table_ref, slice(0, 512), hot)
        centre, other = edge_block(spot, geo, jnp.concatenate([own, own], axis=1), env_n)
        sums = scatter(other, hot)
        oy_ref[0:128] += sums[:, 0:128] + (centre[:, 0:128] + centre[:, 128:256])
        xc_ref[0:128] += sums[:, 128:256]
        oy_ref[128:256] += sums[:, 256:384]
        xc_ref[128:256] += sums[:, 384:512]
        return carry

    lax.fori_loop(0, EDGES // WIDE, main, 0)

    def lone(block, carry):
        spot = pl.ds(pl.multiple_of(EDGES + block * LONE, LONE), LONE)
        geo = geo_ref[:, spot]
        hot_n = one_hot(geo[7:8].astype(jnp.int32), 128)
        hot_c = one_hot(geo[8:9].astype(jnp.int32), 128)
        env_n = fetch(table_ref, slice(128, 256), hot_n)
        env_c = fetch(table_ref, slice(256, 384), hot_c)
        centre, other = edge_block(spot, geo, env_c, env_n)
        xc_ref[0:128] += scatter(other, hot_n)
        oy_ref[128:256] += scatter(centre, hot_c)
        return carry

    lax.fori_loop(0, blocks, lone, 0)


def third_kernel(
    count_ref, odd_ref, one_ref, two_ref, one_in_ref, two_in_ref, dlat_ref, wl_ref, glat_ref, geo_ref, rows_ref, wenv_ref, wbasis_ref,
    yc_ref, ox_ref, table_ref,
):
    own = fill_tables(odd_ref, one_ref, two_ref, one_in_ref, two_in_ref, table_ref)
    blocks = (count_ref[0] + (LONE - 1)) // LONE
    yc_ref[...] = jnp.zeros_like(yc_ref)
    ox_ref[...] = jnp.zeros_like(ox_ref)

    def edge_block(spot, geo, grad_c, grad_n):
        unit = unit_rows(geo)
        envelope, radius = geo[3:4], geo[4:5]
        rows = rows_ref[:, spot]
        plain = wl_ref[:, spot]
        grad_w = 0.25 * (project(grad_c, unit, 1.0) + project(grad_n, unit, -1.0))
        weight = plain * (0.25 * envelope)
        grad_env = rows[0:1] + jnp.sum(grad_w * plain, axis=0, keepdims=True)
        grad_lat = glat_ref[:, spot] + product(wenv_ref[...], grad_w * envelope)
        grad_pre = grad_lat * dlat_ref[:, spot]
        grad_basis = product(wbasis_ref[...], grad_pre)
        basis, gap = basis_of(radius)
        grad_r = jnp.sum(grad_basis * (-8.0 * gap * basis), axis=0, keepdims=True)
        inverse = 1.0 / radius
        along = []
        for comp in range(3):
            lines = slice((comp + 1) * TC, (comp + 2) * TC)
            along.append(rows[2 + comp : 3 + comp] + jnp.sum(weight * (grad_c[lines] - grad_n[lines]), axis=0, keepdims=True))
            grad_r = grad_r - along[comp] * unit[comp] * inverse
        grad_sq = grad_r * (0.5 * inverse) - 0.25 * envelope * grad_env
        force = [-(along[comp] * inverse + 2.0 * radius * unit[comp] * grad_sq) for comp in range(3)]
        line = lax.broadcasted_iota(jnp.int32, (8, envelope.shape[1]), 0)
        packed = jnp.where(line == 3, rows[1:2], 0.0)
        for comp in range(3):
            packed = jnp.where(line == comp, force[comp], packed)
        return packed, jnp.where(line == 3, packed, -packed)

    def main(block, carry):
        spot = pl.ds(pl.multiple_of(block * WIDE, WIDE), WIDE)
        geo = geo_ref[:, spot]
        hot = one_hot(geo[7:8].astype(jnp.int32), 512)
        grad_n = fetch(table_ref, slice(0, 512), hot)
        other, centre = edge_block(spot, geo, jnp.concatenate([own, own], axis=1), grad_n)
        sums = scatter(other, hot)
        ox_ref[0:8] += sums[:, 0:128] + (centre[:, 0:128] + centre[:, 128:256])
        ox_ref[8:16] += sums[:, 128:256]
        yc_ref[0:8] += sums[:, 256:384]
        yc_ref[8:16] += sums[:, 384:512]
        return carry

    lax.fori_loop(0, EDGES // WIDE, main, 0)

    def lone(block, carry):
        spot = pl.ds(pl.multiple_of(EDGES + block * LONE, LONE), LONE)
        geo = geo_ref[:, spot]
        hot_n = one_hot(geo[7:8].astype(jnp.int32), 128)
        hot_c = one_hot(geo[8:9].astype(jnp.int32), 128)
        grad_n = fetch(table_ref, slice(128, 256), hot_n)
        grad_c = fetch(table_ref, slice(256, 384), hot_c)
        other, centre = edge_block(spot, geo, grad_c, grad_n)
        ox_ref[8:16] += scatter(other, hot_n)
        yc_ref[0:8] += scatter(centre, hot_c)
        return carry

    lax.fori_loop(0, blocks, lone, 0)


def call(kernel, out_shape, in_specs, out_specs, scratch, cost):
    return pl.pallas_call(
        kernel,
        out_shape=out_shape,
        in_specs=in_specs,
        out_specs=out_specs,
        scratch_shapes=scratch,
        compiler_params=pltpu.CompilerParams(vmem_limit_bytes=VMEM_LIMIT),
        cost_estimate=pl.CostEstimate(flops=cost, bytes_accessed=1 << 20, transcendentals=1 << 18),
    )


def shape(*dims):
    return jax.ShapeDtypeStruct(dims, F32)


IN_VMEM = pl.BlockSpec(memory_space=pltpu.VMEM)
IN_SMEM = pl.BlockSpec(memory_space=pltpu.SMEM)


BOXES_X, BOXES_Y = 32, 16
RUNGS = [(y, half if y % 2 == 0 else 1 - half) for y in range(8) for half in range(2)]
RUNGS = RUNGS[4:] + RUNGS[:4]
AROUND = {(0, 0): 0, (0, 1): 1, (1, 1): 2, (1, 0): 3}


def at_home(p, q):
    return (p % BOXES_X) * BOXES_Y + q % BOXES_Y


def at_work(p, q):
    chip, core = (p % BOXES_X) // 2, p % 2
    z, left = (chip, 0) if chip < 8 else (15 - chip, 1)
    y, right = RUNGS[q % BOXES_Y]
    x = AROUND[(left, right)]
    return (((y // 4) * 8 + z) * 2 + core) * BOXES_Y + (y % 4) * 4 + x


def odd_box():
    gx, gy = lax.axis_index("gx"), lax.axis_index("gy")
    y = (gx // 16) * 4 + gy // 4
    right = (gy % 4 + 1) // 2
    return gx % 2 == 1, (y + right) % 2 == 1


def move(block, source, target, shift):
    pairs = [
        (source(p + shift[0], q + shift[1]), target(p, q)) for p in range(BOXES_X) for q in range(BOXES_Y)
    ]
    return lax.ppermute(block, ("gx", "gy"), pairs)


def trade(block, axis, first):
    pairs = []
    for p in range(BOXES_X):
        for q in range(BOXES_Y):
            away = 1 if (p, q)[axis] % 2 == first else -1
            pairs.append((at_work(p + away * (axis == 0), q + away * (axis == 1)), at_work(p, q)))
    return lax.ppermute(block, ("gx", "gy"), pairs)


def butterfly(xc, oy, odd_p, odd_q):
    far = jnp.where(odd_p, xc, oy)
    near = jnp.where(odd_p, oy, xc)
    far_in = trade(far, 0, 1)
    near_in = trade(near, 0, 0)
    far, near = far + far_in, near + near_in
    here = jnp.where(odd_p, near, far)
    beside = jnp.where(odd_p, far, near)
    up = jnp.concatenate([here[128:256], beside[128:256]], axis=0)
    down = jnp.concatenate([here[0:128], beside[0:128]], axis=0)
    one = jnp.where(odd_q, up, down)
    two = jnp.where(odd_q, down, up)
    return one, two, trade(one, 1, 1), trade(two, 1, 0)


def local(
    positions, species, neighbours, counts, image_z, send_lists, w_basis, w_center, w_neigh, w_env, w_latent, w_tensor, w_out
):
    base = jnp.concatenate(
        [
            positions[0, 0],
            species[0].astype(F32),
            send_lists[0, 0].reshape(2, ATOMS).astype(F32),
            counts[0].astype(F32),
            jnp.zeros((1, ATOMS), F32),
        ],
        axis=0,
    )
    odd_p, odd_q = odd_box()
    odd = odd_q.astype(jnp.int32).reshape(1)
    in_x = move(base, at_home, at_work, (1, 0))
    own = jnp.concatenate([base, neighbours[0, 0].T.astype(F32), image_z[0, 0].T.astype(F32)], axis=0)
    own = move(own, at_home, at_work, (0, 0))
    in_yc = move(jnp.concatenate([own, in_x], axis=0), at_work, at_work, (0, 1))

    wfeat = jnp.concatenate(
        [w_basis, (w_center[0] + w_neigh[0])[None], (w_center[1] - w_center[0])[None], (w_neigh[1] - w_neigh[0])[None],
         jnp.zeros((5, 128), F32)], axis=0
    ).T
    xc, oy, lat, dlat, wl, geo, count = call(
        first_kernel,
        (shape(256, 128), shape(256, 128), shape(128, 2 * EDGES), shape(128, 2 * EDGES), shape(32, 2 * EDGES),
         shape(16, 2 * EDGES), jax.ShapeDtypeStruct((1,), jnp.int32)),
        [IN_VMEM] * 5,
        (IN_VMEM,) * 6 + (IN_SMEM,),
        [pltpu.VMEM((16, ATOMS), F32)],
        500_000_000,
    )(own, in_x, in_yc, wfeat, w_env.T)
    one, two, one_in, two_in = butterfly(xc, oy, odd_p, odd_q)
    wten = w_tensor.reshape(2 * TC, 128)
    xc, oy, glat, rows = call(
        second_kernel,
        (shape(256, 128), shape(256, 128), shape(128, 2 * EDGES), shape(8, 2 * EDGES)),
        [IN_SMEM] * 2 + [IN_VMEM] * 11,
        (IN_VMEM,) * 4,
        [pltpu.VMEM((256, 512), BF16)],
        1_000_000_000,
    )(count, odd, one, two, one_in, two_in, lat, geo, w_latent.T, w_latent, wten.T, wten, w_out[:, None])
    one, two, one_in, two_in = butterfly(xc, oy, odd_p, odd_q)
    yc, ox = call(
        third_kernel,
        (shape(16, 128), shape(16, 128)),
        [IN_SMEM] * 2 + [IN_VMEM] * 11,
        (IN_VMEM,) * 2,
        [pltpu.VMEM((256, 512), BF16)],
        500_000_000,
    )(count, odd, one, two, one_in, two_in, dlat, wl, glat, geo, rows, w_env, w_basis)
    ox = ox + move(yc, at_work, at_work, (0, -1))
    total = move(ox[8:16], at_work, at_home, (-1, 0)) + move(ox[0:8], at_work, at_home, (0, 0))
    return (total[0:3][None, None], total[3][None, None])


def solution(mesh):
    part = P("gx", "gy", None)
    wide = P("gx", "gy", None, None)
    return jax.shard_map(
        local,
        mesh=mesh,
        in_specs=(wide, part, wide, part, wide, part) + (P(),) * 7,
        out_specs=(wide, part),
        check_vma=False,
    )
```

```python
import jax
import jax.numpy as jnp
from jax import lax
from jax.experimental import pallas as pl
from jax.experimental.pallas import tpu as pltpu
from jax.sharding import PartitionSpec as P

F32 = jnp.float32
BF16 = jnp.bfloat16
ATOMS = 128
SLOTS = 8
EDGES = ATOMS * SLOTS
WIDE = 1024
LONE = 128
TC = 32
VMEM_LIMIT = 24 * 1024 * 1024


def halves(x):
    high = x.astype(BF16)
    return high, (x - high.astype(F32)).astype(BF16)


def dot_nn(a, b):
    return lax.dot_general(a, b, (((1,), (0,)), ((), ())), preferred_element_type=F32)


def dot_nt(a, b):
    return lax.dot_general(a, b, (((1,), (1,)), ((), ())), preferred_element_type=F32)


def product(left, right):
    a, b = halves(left)
    c, d = halves(right)
    return dot_nn(a, c) + (dot_nn(a, d) + dot_nn(b, c))


def one_hot(index_row, rows):
    lines = lax.broadcasted_iota(jnp.int32, (rows, index_row.shape[1]), 0)
    return jnp.where(lines == index_row, 1.0, 0.0).astype(BF16)


def gather(high, low, hot):
    return dot_nn(high, hot) + dot_nn(low, hot)


def scatter(values, hot):
    high, low = halves(values)
    return dot_nt(high, hot) + dot_nt(low, hot)


def fold(values):
    return sum(values[:, k * ATOMS : (k + 1) * ATOMS] for k in range(WIDE // ATOMS))


def lanes(table, index):
    return jnp.take_along_axis(table, index, axis=1, mode="promise_in_bounds")


def spread(row):
    return jnp.broadcast_to(row, (8, row.shape[1]))


def sigmoid_parts(pre):
    gate = 1.0 / (1.0 + jnp.exp(-pre))
    value = pre * gate
    return value, gate + value * (1.0 - gate)


def four(weight, unit, sign):
    parts = [weight]
    for comp in range(3):
        parts.append((sign * weight) * unit[comp])
    return jnp.concatenate(parts, axis=0)


def basis_of(radius):
    step = lax.broadcasted_iota(jnp.int32, (8, radius.shape[1]), 0).astype(F32)
    gap = radius - (0.5 + 2.5 * step / 7.0)
    return jnp.exp(-4.0 * gap * gap), gap


def unit_rows(geo):
    return [geo[0:1], geo[1:2], geo[2:3]]


def geometry(dx, dy, dz, live):
    radius_sq = dx * dx + dy * dy + dz * dz + 0.25
    radius = jnp.sqrt(radius_sq)
    inverse = 1.0 / radius
    envelope = live * jnp.exp(-0.25 * radius_sq)
    return dx * inverse, dy * inverse, dz * inverse, envelope, radius


def pack_kernel(*refs):
    sources, (base_ref, own_ref), held, sems = refs[:6], refs[6:8], refs[8:14], refs[14]
    copies = [pltpu.make_async_copy(source, place, sems.at[i]) for i, (source, place) in enumerate(zip(sources, held))]
    for copy in copies:
        copy.start()
    for copy in copies:
        copy.wait()
    positions, species, counts, sends, neighbours, images = held
    lists = sends[0].astype(F32)
    rows = [positions[0], positions[1], positions[2], species[0].astype(F32), lists[:, 0:ATOMS], lists[:, ATOMS:]]
    rows += [counts[0].astype(F32), jnp.zeros((1, ATOMS), F32)]
    for line, values in enumerate(rows):
        base_ref[line : line + 1] = values
        own_ref[line : line + 1] = values
    own_ref[8:16] = neighbours[...].astype(F32)
    own_ref[16:24] = images[...].astype(F32)


def first_kernel(
    own_ref, x_ref, yc_ref, wfeat_ref, wenv_ref, xc_ref, oy_ref, lat_ref, dlat_ref, wl_ref, geo_ref, count_ref, rank_ref
):
    sub = lax.broadcasted_iota(jnp.int32, (SLOTS, ATOMS), 0)
    lane = lax.broadcasted_iota(jnp.int32, (SLOTS, ATOMS), 1)
    x_send = x_ref[5:6]
    list_low = spread(x_ref[4:5])
    list_high = jnp.where(lane < 64, spread(yc_ref[5:6]), jnp.where(lane < 96, spread(yc_ref[29:30]), spread(x_send)))

    neigh = own_ref[8:16].astype(jnp.int32)
    live = sub < spread(own_ref[6:7]).astype(jnp.int32)
    ghost = neigh - ATOMS
    low = lanes(list_low, jnp.clip(ghost, 0, ATOMS - 1)).astype(jnp.int32)
    high = lanes(list_high, jnp.clip(ghost - ATOMS, 0, ATOMS - 1)).astype(jnp.int32)
    atom = jnp.where(ghost < 0, neigh, jnp.where(ghost < ATOMS, low, high))
    in_x = (ghost >= 0) & (ghost < 128)
    in_y = (ghost >= 128) & (ghost < 192)
    in_c = ghost >= 192
    live = live & (ghost < 224)

    def pick(line):
        values = lanes(spread(own_ref[line : line + 1]), atom)
        values = jnp.where(in_x, lanes(spread(x_ref[line : line + 1]), atom), values)
        values = jnp.where(in_y, lanes(spread(yc_ref[line : line + 1]), atom), values)
        return jnp.where(in_c, lanes(spread(yc_ref[24 + line : 25 + line]), atom), values)

    shift_x = jnp.where(in_x | in_c, 1.0, 0.0)
    shift_y = jnp.where(in_y | in_c, 1.0, 0.0)
    dx = pick(0) + shift_x - own_ref[0:1]
    dy = pick(1) + shift_y - own_ref[1:2]
    dz = pick(2) - own_ref[2:3] + own_ref[16:24]
    rows = list(geometry(dx, dy, dz, jnp.where(live, 1.0, 0.0)))
    rows.append(spread(own_ref[3:4]))
    rows.append(pick(3))
    box = jnp.where(in_x, 128, 0) + jnp.where(in_y, 256, 0) + jnp.where(in_c, 384, 0)
    rows.append((box + atom).astype(F32))
    for line, values in enumerate(rows):
        for k in range(SLOTS):
            geo_ref[line : line + 1, k * ATOMS : (k + 1) * ATOMS] = values[k : k + 1]
    geo_ref[8:16, 0:EDGES] = jnp.zeros((8, EDGES), F32)

    y_neigh = yc_ref[8:16].astype(jnp.int32)
    wanted = (sub < spread(yc_ref[6:7]).astype(jnp.int32)) & (y_neigh >= 352)
    wanted_f = jnp.where(wanted, 1.0, 0.0)
    y_atom = lanes(spread(x_send), jnp.clip(y_neigh - 256, 0, ATOMS - 1))
    before = jnp.where(
        lax.broadcasted_iota(jnp.int32, (ATOMS, ATOMS), 0) <= lax.broadcasted_iota(jnp.int32, (ATOMS, ATOMS), 1), 1.0, 0.0
    ).astype(BF16)
    upto = dot_nn(wanted_f.astype(BF16), before)
    totals = jnp.sum(wanted_f, axis=1, keepdims=True)
    running = jnp.zeros((1, 1), F32)
    starts = []
    for k in range(SLOTS):
        starts.append(running)
        running = running + totals[k : k + 1]
    rank = jnp.where(wanted, upto - 1.0 + jnp.concatenate(starts, axis=0), -1.0)
    rank_ref[0:8] = rank
    rank_ref[8:16] = y_atom
    count = jnp.sum(wanted_f).astype(jnp.int32)
    count_ref[0] = count
    blocks = (count + (LONE - 1)) // LONE

    def compact(block, carry):
        base = (block * LONE).astype(F32)
        line = lax.broadcasted_iota(jnp.int32, (LONE, ATOMS), 0).astype(F32) + base
        packed = jnp.zeros((8, LONE), F32)
        for k in range(SLOTS):
            hot = jnp.where(line == rank_ref[k : k + 1], 1.0, 0.0).astype(BF16)
            feats = jnp.where(sub == 0, lane.astype(F32), 0.0)
            feats = jnp.where(sub == 1, rank_ref[8 + k : 9 + k], feats)
            feats = jnp.where(sub == 2, yc_ref[16 + k : 17 + k], feats)
            feats = jnp.where(sub == 3, 1.0, feats)
            packed = packed + dot_nt(feats.astype(BF16), hot)
        centre = lanes(yc_ref[0:8], spread(packed[0:1]).astype(jnp.int32))
        other = lanes(x_ref[0:8], spread(packed[1:2]).astype(jnp.int32))
        ex = other[0:1] + 1.0 - centre[0:1]
        ey = other[1:2] - 1.0 - centre[1:2]
        ez = other[2:3] - centre[2:3] + packed[2:3]
        found = list(geometry(ex, ey, ez, packed[3:4])) + [centre[3:4], other[3:4], packed[1:2], packed[0:1]]
        spot = pl.ds(pl.multiple_of(EDGES + block * LONE, LONE), LONE)
        for number, values in enumerate(found):
            geo_ref[number : number + 1, spot] = values
        return carry

    lax.fori_loop(0, blocks, compact, 0)

    wfeat = wfeat_ref[...]
    wenv = wenv_ref[...]
    xc_ref[...] = jnp.zeros_like(xc_ref)
    oy_ref[...] = jnp.zeros_like(oy_ref)

    def edge_block(spot):
        geo = geo_ref[:, spot]
        basis, _ = basis_of(geo[4:5])
        line = lax.broadcasted_iota(jnp.int32, basis.shape, 0)
        extra = jnp.where(line == 0, 1.0, jnp.where(line == 1, geo[5:6], jnp.where(line == 2, geo[6:7], 0.0)))
        pre = product(wfeat, jnp.concatenate([basis, extra], axis=0))
        latent, slope = sigmoid_parts(pre)
        lat_ref[:, spot] = latent
        dlat_ref[:, spot] = slope
        plain = product(wenv, latent)
        wl_ref[:, spot] = plain
        weight = plain * (0.25 * geo[3:4])
        unit = unit_rows(geo)
        return geo, four(weight, unit, 1.0), four(weight, unit, -1.0)

    def main(block, carry):
        spot = pl.ds(block * WIDE, WIDE)
        geo, centre, other = edge_block(spot)
        sums = scatter(other, one_hot(geo[7:8].astype(jnp.int32), 512))
        oy_ref[0:128] += sums[:, 0:128] + fold(centre)
        xc_ref[0:128] += sums[:, 128:256]
        oy_ref[128:256] += sums[:, 256:384]
        xc_ref[128:256] += sums[:, 384:512]
        return carry

    for block in range(EDGES // WIDE):
        main(block, 0)

    def lone(block, carry):
        spot = pl.ds(pl.multiple_of(EDGES + block * LONE, LONE), LONE)
        geo, centre, other = edge_block(spot)
        xc_ref[0:128] += scatter(other, one_hot(geo[7:8].astype(jnp.int32), 128))
        oy_ref[128:256] += scatter(centre, one_hot(geo[8:9].astype(jnp.int32), 128))
        return carry

    lax.fori_loop(0, blocks, lone, 0)


def fill_tables(odd_ref, one_ref, two_ref, one_in_ref, two_in_ref, table_ref):
    odd = odd_ref[0] == 1
    one = one_ref[...] + one_in_ref[...]
    two = two_ref[...] + two_in_ref[...]
    down = jnp.where(odd, two, one)
    up = jnp.where(odd, one, two)
    own = down[0:128]
    for place, values in enumerate((own, down[128:256], up[0:128], up[128:256])):
        high, low = halves(values)
        table_ref[0:128, place * 128 : (place + 1) * 128] = high
        table_ref[128:256, place * 128 : (place + 1) * 128] = low
    return own


def fetch(table_ref, spot, hot):
    both = dot_nn(table_ref[:, spot], hot)
    return both[0:128] + both[128:256]


def project(rows, unit, sign):
    total = rows[0:TC]
    for comp in range(3):
        total = total + (sign * unit[comp]) * rows[(comp + 1) * TC : (comp + 2) * TC]
    return total


def early_kernel(count_ref, lat_ref, wlat_t_ref, wout_ref, pre_ref, read_ref):
    blocks = (count_ref[0] + (LONE - 1)) // LONE
    wout = wout_ref[...]

    def edge_block(spot):
        latent = lat_ref[:, spot]
        pre_ref[:, spot] = product(wlat_t_ref[...], latent)
        read_ref[0:1, spot] = jnp.sum(wout * latent, axis=0, keepdims=True)

    edge_block(pl.ds(0, EDGES))

    def lone(block, carry):
        edge_block(pl.ds(pl.multiple_of(EDGES + block * LONE, LONE), LONE))
        return carry

    lax.fori_loop(0, blocks, lone, 0)


def late_kernel(count_ref, gpre_ref, geo_ref, wlat_ref, wout_ref, glat_ref):
    blocks = (count_ref[0] + (LONE - 1)) // LONE

    def edge_block(spot):
        glat_ref[:, spot] = wout_ref[...] * geo_ref[3:4, spot] + product(wlat_ref[...], gpre_ref[:, spot])

    edge_block(pl.ds(0, EDGES))

    def lone(block, carry):
        edge_block(pl.ds(pl.multiple_of(EDGES + block * LONE, LONE), LONE))
        return carry

    lax.fori_loop(0, blocks, lone, 0)


def second_kernel(
    count_ref, odd_ref, one_ref, two_ref, one_in_ref, two_in_ref, early_ref, first_read_ref, geo_ref, wten_t_ref, wten_ref, wout_ref,
    xc_ref, oy_ref, gpre_ref, rows_ref, table_ref,
):
    own = fill_tables(odd_ref, one_ref, two_ref, one_in_ref, two_in_ref, table_ref)
    blocks = (count_ref[0] + (LONE - 1)) // LONE
    wout = wout_ref[...]
    xc_ref[...] = jnp.zeros_like(xc_ref)
    oy_ref[...] = jnp.zeros_like(oy_ref)

    def edge_block(spot, geo, env_c, env_n):
        unit = unit_rows(geo)
        envelope = geo[3:4]
        both = jnp.concatenate([project(env_c, unit, 1.0), project(env_n, unit, -1.0)], axis=0)
        pre = early_ref[:, spot] + product(wten_t_ref[...], both)
        hidden, slope = sigmoid_parts(pre)
        read = first_read_ref[0:1, spot] + jnp.sum(wout * hidden, axis=0, keepdims=True)
        grad_pre = (wout * envelope) * slope
        gpre_ref[:, spot] = grad_pre
        grad_both = product(wten_ref[...], grad_pre)
        grad_c, grad_n = grad_both[0:TC], grad_both[TC : 2 * TC]
        found = [read, 0.5 * envelope * read]
        for comp in range(3):
            lines = slice((comp + 1) * TC, (comp + 2) * TC)
            found.append(jnp.sum(env_c[lines] * grad_c - env_n[lines] * grad_n, axis=0, keepdims=True))
        for number, values in enumerate(found):
            rows_ref[number : number + 1, spot] = values
        return four(grad_c, unit, 1.0), four(grad_n, unit, -1.0)

    def main(block, carry):
        spot = pl.ds(block * WIDE, WIDE)
        geo = geo_ref[:, spot]
        hot = one_hot(geo[7:8].astype(jnp.int32), 512)
        env_n = fetch(table_ref, slice(0, 512), hot)
        centre, other = edge_block(spot, geo, jnp.concatenate([own] * (WIDE // ATOMS), axis=1), env_n)
        sums = scatter(other, hot)
        oy_ref[0:128] += sums[:, 0:128] + fold(centre)
        xc_ref[0:128] += sums[:, 128:256]
        oy_ref[128:256] += sums[:, 256:384]
        xc_ref[128:256] += sums[:, 384:512]
        return carry

    for block in range(EDGES // WIDE):
        main(block, 0)

    def lone(block, carry):
        spot = pl.ds(pl.multiple_of(EDGES + block * LONE, LONE), LONE)
        geo = geo_ref[:, spot]
        hot_n = one_hot(geo[7:8].astype(jnp.int32), 128)
        hot_c = one_hot(geo[8:9].astype(jnp.int32), 128)
        env_n = fetch(table_ref, slice(128, 256), hot_n)
        env_c = fetch(table_ref, slice(256, 384), hot_c)
        centre, other = edge_block(spot, geo, env_c, env_n)
        xc_ref[0:128] += scatter(other, hot_n)
        oy_ref[128:256] += scatter(centre, hot_c)
        return carry

    lax.fori_loop(0, blocks, lone, 0)


def third_kernel(
    count_ref, odd_ref, one_ref, two_ref, one_in_ref, two_in_ref, dlat_ref, wl_ref, glat_ref, geo_ref, rows_ref, wenv_ref, wbasis_ref,
    yc_ref, ox_ref, table_ref,
):
    own = fill_tables(odd_ref, one_ref, two_ref, one_in_ref, two_in_ref, table_ref)
    blocks = (count_ref[0] + (LONE - 1)) // LONE
    yc_ref[...] = jnp.zeros_like(yc_ref)
    ox_ref[...] = jnp.zeros_like(ox_ref)

    def edge_block(spot, geo, grad_c, grad_n):
        unit = unit_rows(geo)
        envelope, radius = geo[3:4], geo[4:5]
        rows = rows_ref[:, spot]
        plain = wl_ref[:, spot]
        grad_w = 0.25 * (project(grad_c, unit, 1.0) + project(grad_n, unit, -1.0))
        weight = plain * (0.25 * envelope)
        grad_env = rows[0:1] + jnp.sum(grad_w * plain, axis=0, keepdims=True)
        grad_lat = glat_ref[:, spot] + product(wenv_ref[...], grad_w * envelope)
        grad_pre = grad_lat * dlat_ref[:, spot]
        grad_basis = product(wbasis_ref[...], grad_pre)
        basis, gap = basis_of(radius)
        grad_r = jnp.sum(grad_basis * (-8.0 * gap * basis), axis=0, keepdims=True)
        inverse = 1.0 / radius
        along = []
        for comp in range(3):
            lines = slice((comp + 1) * TC, (comp + 2) * TC)
            along.append(rows[2 + comp : 3 + comp] + jnp.sum(weight * (grad_c[lines] - grad_n[lines]), axis=0, keepdims=True))
            grad_r = grad_r - along[comp] * unit[comp] * inverse
        grad_sq = grad_r * (0.5 * inverse) - 0.25 * envelope * grad_env
        force = [-(along[comp] * inverse + 2.0 * radius * unit[comp] * grad_sq) for comp in range(3)]
        line = lax.broadcasted_iota(jnp.int32, (8, envelope.shape[1]), 0)
        packed = jnp.where(line == 3, rows[1:2], 0.0)
        for comp in range(3):
            packed = jnp.where(line == comp, force[comp], packed)
        return packed, jnp.where(line == 3, packed, -packed)

    def main(block, carry):
        spot = pl.ds(block * WIDE, WIDE)
        geo = geo_ref[:, spot]
        hot = one_hot(geo[7:8].astype(jnp.int32), 512)
        grad_n = fetch(table_ref, slice(0, 512), hot)
        other, centre = edge_block(spot, geo, jnp.concatenate([own] * (WIDE // ATOMS), axis=1), grad_n)
        sums = scatter(other, hot)
        ox_ref[0:8] += sums[:, 0:128] + fold(centre)
        ox_ref[8:16] += sums[:, 128:256]
        yc_ref[0:8] += sums[:, 256:384]
        yc_ref[8:16] += sums[:, 384:512]
        return carry

    for block in range(EDGES // WIDE):
        main(block, 0)

    def lone(block, carry):
        spot = pl.ds(pl.multiple_of(EDGES + block * LONE, LONE), LONE)
        geo = geo_ref[:, spot]
        hot_n = one_hot(geo[7:8].astype(jnp.int32), 128)
        hot_c = one_hot(geo[8:9].astype(jnp.int32), 128)
        grad_n = fetch(table_ref, slice(128, 256), hot_n)
        grad_c = fetch(table_ref, slice(256, 384), hot_c)
        other, centre = edge_block(spot, geo, grad_c, grad_n)
        ox_ref[8:16] += scatter(other, hot_n)
        yc_ref[0:8] += scatter(centre, hot_c)
        return carry

    lax.fori_loop(0, blocks, lone, 0)


def call(kernel, out_shape, in_specs, out_specs, scratch, cost, limit=VMEM_LIMIT):
    return pl.pallas_call(
        kernel,
        out_shape=out_shape,
        in_specs=in_specs,
        out_specs=out_specs,
        scratch_shapes=scratch,
        compiler_params=pltpu.CompilerParams(vmem_limit_bytes=limit),
        cost_estimate=pl.CostEstimate(flops=cost, bytes_accessed=1 << 20, transcendentals=1 << 18),
    )


def shape(*dims):
    return jax.ShapeDtypeStruct(dims, F32)


IN_VMEM = pl.BlockSpec(memory_space=pltpu.VMEM)
IN_SMEM = pl.BlockSpec(memory_space=pltpu.SMEM)


BOXES_X, BOXES_Y = 32, 16
RUNGS = [(y, half if y % 2 == 0 else 1 - half) for y in range(8) for half in range(2)]
RUNGS = RUNGS[4:] + RUNGS[:4]
AROUND = {(0, 0): 0, (0, 1): 1, (1, 1): 2, (1, 0): 3}


def at_home(p, q):
    return (p % BOXES_X) * BOXES_Y + q % BOXES_Y


def at_work(p, q):
    chip, core = (p % BOXES_X) // 2, p % 2
    z, left = (chip, 0) if chip < 8 else (15 - chip, 1)
    y, right = RUNGS[q % BOXES_Y]
    x = AROUND[(left, right)]
    return (((y // 4) * 8 + z) * 2 + core) * BOXES_Y + (y % 4) * 4 + x


def odd_box():
    gx, gy = lax.axis_index("gx"), lax.axis_index("gy")
    y = (gx // 16) * 4 + gy // 4
    right = (gy % 4 + 1) // 2
    return gx % 2 == 1, (y + right) % 2 == 1


def move(block, source, target, shift):
    pairs = [
        (source(p + shift[0], q + shift[1]), target(p, q)) for p in range(BOXES_X) for q in range(BOXES_Y)
    ]
    return lax.ppermute(block, ("gx", "gy"), pairs)


def trade(block, axis, first):
    pairs = []
    for p in range(BOXES_X):
        for q in range(BOXES_Y):
            away = 1 if (p, q)[axis] % 2 == first else -1
            pairs.append((at_work(p + away * (axis == 0), q + away * (axis == 1)), at_work(p, q)))
    return lax.ppermute(block, ("gx", "gy"), pairs)


def butterfly(xc, oy, odd_p, odd_q):
    far = jnp.where(odd_p, xc, oy)
    near = jnp.where(odd_p, oy, xc)
    near_in = trade(near, 0, 0)
    far_in = trade(far, 0, 1)
    far, near = far + far_in, near + near_in
    here = jnp.where(odd_p, near, far)
    beside = jnp.where(odd_p, far, near)
    up = jnp.concatenate([here[128:256], beside[128:256]], axis=0)
    down = jnp.concatenate([here[0:128], beside[0:128]], axis=0)
    one = jnp.where(odd_q, up, down)
    two = jnp.where(odd_q, down, up)
    return one, two, trade(one, 1, 1), trade(two, 1, 0)


def local(
    positions, species, neighbours, counts, image_z, send_lists, w_basis, w_center, w_neigh, w_env, w_latent, w_tensor, w_out
):
    base, own = call(
        pack_kernel,
        (shape(8, ATOMS), shape(24, ATOMS)),
        [pl.BlockSpec(memory_space=pl.ANY)] * 6,
        (IN_VMEM,) * 2,
        [
            pltpu.VMEM((3, 1, ATOMS), F32),
            pltpu.VMEM((1, 1, ATOMS), jnp.int32),
            pltpu.VMEM((1, 1, ATOMS), jnp.int32),
            pltpu.VMEM((1, 1, 2 * ATOMS), jnp.int32),
            pltpu.VMEM((SLOTS, ATOMS), jnp.int32),
            pltpu.VMEM((SLOTS, ATOMS), jnp.int32),
            pltpu.SemaphoreType.DMA((6,)),
        ],
        1000,
        60 * 1024 * 1024,
    )(
        positions.transpose(0, 2, 1, 3).reshape(3, 1, ATOMS),
        species,
        counts,
        send_lists,
        neighbours.transpose(0, 1, 3, 2).reshape(SLOTS, ATOMS),
        image_z.transpose(0, 1, 3, 2).reshape(SLOTS, ATOMS),
    )
    odd_p, odd_q = odd_box()
    odd = odd_q.astype(jnp.int32).reshape(1)
    in_x = move(base, at_home, at_work, (1, 0))
    own = move(own, at_home, at_work, (0, 0))
    in_yc = move(jnp.concatenate([own, in_x], axis=0), at_work, at_work, (0, 1))

    wfeat = jnp.concatenate(
        [w_basis, (w_center[0] + w_neigh[0])[None], (w_center[1] - w_center[0])[None], (w_neigh[1] - w_neigh[0])[None],
         jnp.zeros((5, 128), F32)], axis=0
    ).T
    xc, oy, lat, dlat, wl, geo, count = call(
        first_kernel,
        (shape(256, 128), shape(256, 128), shape(128, 2 * EDGES), shape(128, 2 * EDGES), shape(32, 2 * EDGES),
         shape(16, 2 * EDGES), jax.ShapeDtypeStruct((1,), jnp.int32)),
        [IN_VMEM] * 5,
        (IN_VMEM,) * 6 + (IN_SMEM,),
        [pltpu.VMEM((16, ATOMS), F32)],
        500_000_000,
    )(own, in_x, in_yc, wfeat, w_env.T)
    one, two, one_in, two_in = butterfly(xc, oy, odd_p, odd_q)
    wten = w_tensor.reshape(2 * TC, 128)
    wout = w_out[:, None]
    early, first_read = call(
        early_kernel,
        (shape(128, 2 * EDGES), shape(8, 2 * EDGES)),
        [IN_SMEM] + [IN_VMEM] * 3,
        (IN_VMEM,) * 2,
        [],
        200_000_000,
    )(count, lat, w_latent.T, wout)
    xc, oy, gpre, rows = call(
        second_kernel,
        (shape(256, 128), shape(256, 128), shape(128, 2 * EDGES), shape(8, 2 * EDGES)),
        [IN_SMEM] * 2 + [IN_VMEM] * 10,
        (IN_VMEM,) * 4,
        [pltpu.VMEM((256, 512), BF16)],
        1_000_000_000,
    )(count, odd, one, two, one_in, two_in, early, first_read, geo, wten.T, wten, wout)
    glat = call(
        late_kernel,
        shape(128, 2 * EDGES),
        [IN_SMEM] + [IN_VMEM] * 4,
        IN_VMEM,
        [],
        200_000_000,
    )(count, gpre, geo, w_latent, wout)
    one, two, one_in, two_in = butterfly(xc, oy, odd_p, odd_q)
    yc, ox = call(
        third_kernel,
        (shape(16, 128), shape(16, 128)),
        [IN_SMEM] * 2 + [IN_VMEM] * 11,
        (IN_VMEM,) * 2,
        [pltpu.VMEM((256, 512), BF16)],
        500_000_000,
    )(count, odd, one, two, one_in, two_in, dlat, wl, glat, geo, rows, w_env, w_basis)
    ox = ox + move(yc, at_work, at_work, (0, -1))
    total = move(ox[8:16], at_work, at_home, (-1, 0)) + move(ox[0:8], at_work, at_home, (0, 0))
    return (total[0:3][None, None], total[3][None, None])


def solution(mesh):
    part = P("gx", "gy", None)
    wide = P("gx", "gy", None, None)
    return jax.shard_map(
        local,
        mesh=mesh,
        in_specs=(wide, part, wide, part, wide, part) + (P(),) * 7,
        out_specs=(wide, part),
        check_vma=False,
    )
```

```python
import jax
import jax.numpy as jnp
from jax import lax
from jax.experimental import pallas as pl
from jax.experimental.pallas import tpu as pltpu
from jax.sharding import PartitionSpec as P

F32 = jnp.float32
BF16 = jnp.bfloat16
ATOMS = 128
SLOTS = 8
EDGES = ATOMS * SLOTS
LONE = 128
WIDE = EDGES + LONE
TC = 32
VMEM_LIMIT = 24 * 1024 * 1024


def halves(x):
    high = x.astype(BF16)
    return high, (x - high.astype(F32)).astype(BF16)


def dot_nn(a, b):
    return lax.dot_general(a, b, (((1,), (0,)), ((), ())), preferred_element_type=F32)


def dot_nt(a, b):
    return lax.dot_general(a, b, (((1,), (1,)), ((), ())), preferred_element_type=F32)


def product(left, right):
    a, b = halves(left)
    c, d = halves(right)
    rows = left.shape[0]
    both = dot_nn(jnp.concatenate([a, b], axis=0), c)
    return both[0:rows] + (both[rows:] + dot_nn(a, d))


def one_hot(index_row, rows):
    lines = lax.broadcasted_iota(jnp.int32, (rows, index_row.shape[1]), 0)
    return jnp.where(lines == index_row, 1.0, 0.0).astype(BF16)


def scatter(values, hot):
    rows = values.shape[0]
    both = dot_nt(jnp.concatenate(halves(values), axis=0), hot)
    return both[0:rows] + both[rows:]


def fold(values):
    return sum(values[:, k * ATOMS : (k + 1) * ATOMS] for k in range(SLOTS))


def lanes(table, index):
    return jnp.take_along_axis(table, index, axis=1, mode="promise_in_bounds")


def spread(row):
    return jnp.broadcast_to(row, (8, row.shape[1]))


def sigmoid_parts(pre):
    gate = 1.0 / (1.0 + jnp.exp(-pre))
    value = pre * gate
    return value, gate + value * (1.0 - gate)


def four(weight, unit, sign):
    parts = [weight]
    for comp in range(3):
        parts.append((sign * weight) * unit[comp])
    return jnp.concatenate(parts, axis=0)


def basis_of(radius):
    step = lax.broadcasted_iota(jnp.int32, (8, radius.shape[1]), 0).astype(F32)
    gap = radius - (0.5 + 2.5 * step / 7.0)
    return jnp.exp(-4.0 * gap * gap), gap


def unit_rows(geo):
    return [geo[0:1], geo[1:2], geo[2:3]]


def geometry(dx, dy, dz, live):
    radius_sq = dx * dx + dy * dy + dz * dz + 0.25
    radius = jnp.sqrt(radius_sq)
    inverse = 1.0 / radius
    envelope = live * jnp.exp(-0.25 * radius_sq)
    return dx * inverse, dy * inverse, dz * inverse, envelope, radius


def pack_kernel(*refs):
    sources, own_ref, held, sems = refs[:6], refs[6], refs[7:13], refs[13]
    copies = [pltpu.make_async_copy(source, place, sems.at[i]) for i, (source, place) in enumerate(zip(sources, held))]
    for copy in copies:
        copy.start()
    for copy in copies:
        copy.wait()
    positions, species, counts, sends, neighbours, images = held
    lists = sends[0].astype(F32)
    rows = [positions[0], positions[1], positions[2], species[0].astype(F32), lists[:, 0:ATOMS], lists[:, ATOMS:]]
    rows += [counts[0].astype(F32), jnp.zeros((1, ATOMS), F32)]
    for line, values in enumerate(rows):
        own_ref[line : line + 1] = values
    own_ref[8:16] = neighbours[...].astype(F32)
    own_ref[16:24] = images[...].astype(F32)


def first_kernel(
    own_ref, x_ref, yc_ref, wfeat_ref, wenv_ref, xc_ref, oy_ref, lat_ref, dlat_ref, wl_ref, geo_ref, count_ref, rank_ref
):
    sub = lax.broadcasted_iota(jnp.int32, (SLOTS, ATOMS), 0)
    lane = lax.broadcasted_iota(jnp.int32, (SLOTS, ATOMS), 1)
    x_send = x_ref[5:6]
    list_low = spread(x_ref[4:5])
    list_high = jnp.where(lane < 64, spread(yc_ref[5:6]), jnp.where(lane < 96, spread(yc_ref[29:30]), spread(x_send)))

    neigh = own_ref[8:16].astype(jnp.int32)
    live = sub < spread(own_ref[6:7]).astype(jnp.int32)
    ghost = neigh - ATOMS
    low = lanes(list_low, jnp.clip(ghost, 0, ATOMS - 1)).astype(jnp.int32)
    high = lanes(list_high, jnp.clip(ghost - ATOMS, 0, ATOMS - 1)).astype(jnp.int32)
    atom = jnp.where(ghost < 0, neigh, jnp.where(ghost < ATOMS, low, high))
    in_x = (ghost >= 0) & (ghost < 128)
    in_y = (ghost >= 128) & (ghost < 192)
    in_c = ghost >= 192
    live = live & (ghost < 224)

    def pick(line):
        values = lanes(spread(own_ref[line : line + 1]), atom)
        values = jnp.where(in_x, lanes(spread(x_ref[line : line + 1]), atom), values)
        values = jnp.where(in_y, lanes(spread(yc_ref[line : line + 1]), atom), values)
        return jnp.where(in_c, lanes(spread(yc_ref[24 + line : 25 + line]), atom), values)

    shift_x = jnp.where(in_x | in_c, 1.0, 0.0)
    shift_y = jnp.where(in_y | in_c, 1.0, 0.0)
    dx = pick(0) + shift_x - own_ref[0:1]
    dy = pick(1) + shift_y - own_ref[1:2]
    dz = pick(2) - own_ref[2:3] + own_ref[16:24]
    rows = list(geometry(dx, dy, dz, jnp.where(live, 1.0, 0.0)))
    rows.append(spread(own_ref[3:4]))
    rows.append(pick(3))
    box = jnp.where(in_x, 128, 0) + jnp.where(in_y, 256, 0) + jnp.where(in_c, 384, 0)
    rows.append((box + atom).astype(F32))
    for line, values in enumerate(rows):
        for k in range(SLOTS):
            geo_ref[line : line + 1, k * ATOMS : (k + 1) * ATOMS] = values[k : k + 1]
    geo_ref[8:16, 0:WIDE] = jnp.zeros((8, WIDE), F32)

    y_neigh = yc_ref[8:16].astype(jnp.int32)
    wanted = (sub < spread(yc_ref[6:7]).astype(jnp.int32)) & (y_neigh >= 352)
    wanted_f = jnp.where(wanted, 1.0, 0.0)
    y_atom = lanes(spread(x_send), jnp.clip(y_neigh - 256, 0, ATOMS - 1))
    before = jnp.where(
        lax.broadcasted_iota(jnp.int32, (ATOMS, ATOMS), 0) <= lax.broadcasted_iota(jnp.int32, (ATOMS, ATOMS), 1), 1.0, 0.0
    ).astype(BF16)
    upto = dot_nn(wanted_f.astype(BF16), before)
    totals = jnp.sum(wanted_f, axis=1, keepdims=True)
    running = jnp.zeros((1, 1), F32)
    starts = []
    for k in range(SLOTS):
        starts.append(running)
        running = running + totals[k : k + 1]
    rank = jnp.where(wanted, upto - 1.0 + jnp.concatenate(starts, axis=0), -1.0)
    rank_ref[0:8] = rank
    rank_ref[8:16] = y_atom
    count = jnp.sum(wanted_f).astype(jnp.int32)
    count_ref[0] = count
    blocks = (count + (LONE - 1)) // LONE

    def compact(block, carry):
        base = (block * LONE).astype(F32)
        line = lax.broadcasted_iota(jnp.int32, (LONE, ATOMS), 0).astype(F32) + base
        packed = jnp.zeros((8, LONE), F32)
        for k in range(SLOTS):
            hot = jnp.where(line == rank_ref[k : k + 1], 1.0, 0.0).astype(BF16)
            feats = jnp.where(sub == 0, lane.astype(F32), 0.0)
            feats = jnp.where(sub == 1, rank_ref[8 + k : 9 + k], feats)
            feats = jnp.where(sub == 2, yc_ref[16 + k : 17 + k], feats)
            feats = jnp.where(sub == 3, 1.0, feats)
            packed = packed + dot_nt(feats.astype(BF16), hot)
        centre = lanes(yc_ref[0:8], spread(packed[0:1]).astype(jnp.int32))
        other = lanes(x_ref[0:8], spread(packed[1:2]).astype(jnp.int32))
        ex = other[0:1] + 1.0 - centre[0:1]
        ey = other[1:2] - 1.0 - centre[1:2]
        ez = other[2:3] - centre[2:3] + packed[2:3]
        found = list(geometry(ex, ey, ez, packed[3:4])) + [centre[3:4], other[3:4], packed[1:2] + 128.0, packed[0:1]]
        spot = pl.ds(pl.multiple_of(EDGES + block * LONE, LONE), LONE)
        for number, values in enumerate(found):
            geo_ref[number : number + 1, spot] = values
        return carry

    compact(jnp.int32(0), 0)
    lax.fori_loop(1, blocks, compact, 0)

    wfeat = wfeat_ref[...]
    wenv = wenv_ref[...]

    def edge_block(spot):
        geo = geo_ref[:, spot]
        basis, _ = basis_of(geo[4:5])
        line = lax.broadcasted_iota(jnp.int32, basis.shape, 0)
        extra = jnp.where(line == 0, 1.0, jnp.where(line == 1, geo[5:6], jnp.where(line == 2, geo[6:7], 0.0)))
        pre = product(wfeat, jnp.concatenate([basis, extra], axis=0))
        latent, slope = sigmoid_parts(pre)
        lat_ref[:, spot] = latent
        dlat_ref[:, spot] = slope
        plain = product(wenv, latent)
        wl_ref[:, spot] = plain
        weight = plain * (0.25 * geo[3:4])
        unit = unit_rows(geo)
        return geo, four(weight, unit, 1.0), four(weight, unit, -1.0)

    spot = pl.ds(0, WIDE)
    geo, centre, other = edge_block(spot)
    sums = scatter(other, one_hot(geo[7:8].astype(jnp.int32), 512))
    oy_ref[0:128] = sums[:, 0:128] + fold(centre)
    xc_ref[0:128] = sums[:, 128:256]
    oy_ref[128:256] = sums[:, 256:384] + scatter(centre[:, EDGES:], one_hot(geo[8:9, EDGES:].astype(jnp.int32), 128))
    xc_ref[128:256] = sums[:, 384:512]

    def lone(block, carry):
        spot = pl.ds(pl.multiple_of(EDGES + block * LONE, LONE), LONE)
        geo, centre, other = edge_block(spot)
        xc_ref[0:128] += scatter(other, one_hot(geo[7:8].astype(jnp.int32) - 128, 128))
        oy_ref[128:256] += scatter(centre, one_hot(geo[8:9].astype(jnp.int32), 128))
        return carry

    lax.fori_loop(1, blocks, lone, 0)


def fill_tables(odd_ref, one_ref, two_ref, one_in_ref, two_in_ref, table_ref):
    odd = odd_ref[0] == 1
    one = one_ref[...] + one_in_ref[...]
    two = two_ref[...] + two_in_ref[...]
    down = jnp.where(odd, two, one)
    up = jnp.where(odd, one, two)
    own = down[0:128]
    for place, values in enumerate((own, down[128:256], up[0:128], up[128:256])):
        high, low = halves(values)
        table_ref[0:128, place * 128 : (place + 1) * 128] = high
        table_ref[128:256, place * 128 : (place + 1) * 128] = low
    return own


def fetch(table_ref, spot, hot):
    both = dot_nn(table_ref[:, spot], hot)
    return both[0:128] + both[128:256]


def project(rows, unit, sign):
    total = rows[0:TC]
    for comp in range(3):
        total = total + (sign * unit[comp]) * rows[(comp + 1) * TC : (comp + 2) * TC]
    return total


def early_kernel(count_ref, lat_ref, wlat_t_ref, wout_ref, pre_ref, read_ref):
    blocks = (count_ref[0] + (LONE - 1)) // LONE
    wout = wout_ref[...]

    def edge_block(spot):
        latent = lat_ref[:, spot]
        pre_ref[:, spot] = product(wlat_t_ref[...], latent)
        read_ref[0:1, spot] = jnp.sum(wout * latent, axis=0, keepdims=True)

    edge_block(pl.ds(0, WIDE))

    def lone(block, carry):
        edge_block(pl.ds(pl.multiple_of(EDGES + block * LONE, LONE), LONE))
        return carry

    lax.fori_loop(1, blocks, lone, 0)


def late_kernel(count_ref, gpre_ref, geo_ref, wlat_ref, wout_ref, glat_ref):
    blocks = (count_ref[0] + (LONE - 1)) // LONE

    def edge_block(spot):
        glat_ref[:, spot] = wout_ref[...] * geo_ref[3:4, spot] + product(wlat_ref[...], gpre_ref[:, spot])

    edge_block(pl.ds(0, WIDE))

    def lone(block, carry):
        edge_block(pl.ds(pl.multiple_of(EDGES + block * LONE, LONE), LONE))
        return carry

    lax.fori_loop(1, blocks, lone, 0)


def second_kernel(
    count_ref, odd_ref, one_ref, two_ref, one_in_ref, two_in_ref, early_ref, first_read_ref, geo_ref, wten_t_ref, wten_ref, wout_ref,
    xc_ref, oy_ref, gpre_ref, rows_ref, table_ref,
):
    own = fill_tables(odd_ref, one_ref, two_ref, one_in_ref, two_in_ref, table_ref)
    blocks = (count_ref[0] + (LONE - 1)) // LONE
    wout = wout_ref[...]

    def edge_block(spot, geo, env_c, env_n):
        unit = unit_rows(geo)
        envelope = geo[3:4]
        both = jnp.concatenate([project(env_c, unit, 1.0), project(env_n, unit, -1.0)], axis=0)
        pre = early_ref[:, spot] + product(wten_t_ref[...], both)
        hidden, slope = sigmoid_parts(pre)
        read = first_read_ref[0:1, spot] + jnp.sum(wout * hidden, axis=0, keepdims=True)
        grad_pre = (wout * envelope) * slope
        gpre_ref[:, spot] = grad_pre
        grad_both = product(wten_ref[...], grad_pre)
        grad_c, grad_n = grad_both[0:TC], grad_both[TC : 2 * TC]
        found = [read, 0.5 * envelope * read]
        for comp in range(3):
            lines = slice((comp + 1) * TC, (comp + 2) * TC)
            found.append(jnp.sum(env_c[lines] * grad_c - env_n[lines] * grad_n, axis=0, keepdims=True))
        for number, values in enumerate(found):
            rows_ref[number : number + 1, spot] = values
        return four(grad_c, unit, 1.0), four(grad_n, unit, -1.0)

    spot = pl.ds(0, WIDE)
    geo = geo_ref[:, spot]
    hot = one_hot(geo[7:8].astype(jnp.int32), 512)
    hot_c = one_hot(geo[8:9, EDGES:].astype(jnp.int32), 128)
    env_n = fetch(table_ref, slice(0, 512), hot)
    env_c = jnp.concatenate([own] * SLOTS + [fetch(table_ref, slice(256, 384), hot_c)], axis=1)
    centre, other = edge_block(spot, geo, env_c, env_n)
    sums = scatter(other, hot)
    oy_ref[0:128] = sums[:, 0:128] + fold(centre)
    xc_ref[0:128] = sums[:, 128:256]
    oy_ref[128:256] = sums[:, 256:384] + scatter(centre[:, EDGES:], hot_c)
    xc_ref[128:256] = sums[:, 384:512]

    def lone(block, carry):
        spot = pl.ds(pl.multiple_of(EDGES + block * LONE, LONE), LONE)
        geo = geo_ref[:, spot]
        hot_n = one_hot(geo[7:8].astype(jnp.int32) - 128, 128)
        hot_c = one_hot(geo[8:9].astype(jnp.int32), 128)
        env_n = fetch(table_ref, slice(128, 256), hot_n)
        env_c = fetch(table_ref, slice(256, 384), hot_c)
        centre, other = edge_block(spot, geo, env_c, env_n)
        xc_ref[0:128] += scatter(other, hot_n)
        oy_ref[128:256] += scatter(centre, hot_c)
        return carry

    lax.fori_loop(1, blocks, lone, 0)


def third_kernel(
    count_ref, odd_ref, one_ref, two_ref, one_in_ref, two_in_ref, dlat_ref, wl_ref, glat_ref, geo_ref, rows_ref, wenv_ref, wbasis_ref,
    yc_ref, ox_ref, table_ref,
):
    own = fill_tables(odd_ref, one_ref, two_ref, one_in_ref, two_in_ref, table_ref)
    blocks = (count_ref[0] + (LONE - 1)) // LONE

    def edge_block(spot, geo, grad_c, grad_n):
        unit = unit_rows(geo)
        envelope, radius = geo[3:4], geo[4:5]
        rows = rows_ref[:, spot]
        plain = wl_ref[:, spot]
        grad_w = 0.25 * (project(grad_c, unit, 1.0) + project(grad_n, unit, -1.0))
        weight = plain * (0.25 * envelope)
        grad_env = rows[0:1] + jnp.sum(grad_w * plain, axis=0, keepdims=True)
        grad_lat = glat_ref[:, spot] + product(wenv_ref[...], grad_w * envelope)
        grad_pre = grad_lat * dlat_ref[:, spot]
        grad_basis = product(wbasis_ref[...], grad_pre)
        basis, gap = basis_of(radius)
        grad_r = jnp.sum(grad_basis * (-8.0 * gap * basis), axis=0, keepdims=True)
        inverse = 1.0 / radius
        along = []
        for comp in range(3):
            lines = slice((comp + 1) * TC, (comp + 2) * TC)
            along.append(rows[2 + comp : 3 + comp] + jnp.sum(weight * (grad_c[lines] - grad_n[lines]), axis=0, keepdims=True))
            grad_r = grad_r - along[comp] * unit[comp] * inverse
        grad_sq = grad_r * (0.5 * inverse) - 0.25 * envelope * grad_env
        force = [-(along[comp] * inverse + 2.0 * radius * unit[comp] * grad_sq) for comp in range(3)]
        line = lax.broadcasted_iota(jnp.int32, (8, envelope.shape[1]), 0)
        packed = jnp.where(line == 3, rows[1:2], 0.0)
        for comp in range(3):
            packed = jnp.where(line == comp, force[comp], packed)
        return packed, jnp.where(line == 3, packed, -packed)

    spot = pl.ds(0, WIDE)
    geo = geo_ref[:, spot]
    hot = one_hot(geo[7:8].astype(jnp.int32), 512)
    hot_c = one_hot(geo[8:9, EDGES:].astype(jnp.int32), 128)
    grad_n = fetch(table_ref, slice(0, 512), hot)
    grad_c = jnp.concatenate([own] * SLOTS + [fetch(table_ref, slice(256, 384), hot_c)], axis=1)
    other, centre = edge_block(spot, geo, grad_c, grad_n)
    sums = scatter(other, hot)
    ox_ref[0:8] = sums[:, 0:128] + fold(centre)
    ox_ref[8:16] = sums[:, 128:256]
    yc_ref[0:8] = sums[:, 256:384] + scatter(centre[:, EDGES:], hot_c)
    yc_ref[8:16] = sums[:, 384:512]

    def lone(block, carry):
        spot = pl.ds(pl.multiple_of(EDGES + block * LONE, LONE), LONE)
        geo = geo_ref[:, spot]
        hot_n = one_hot(geo[7:8].astype(jnp.int32) - 128, 128)
        hot_c = one_hot(geo[8:9].astype(jnp.int32), 128)
        grad_n = fetch(table_ref, slice(128, 256), hot_n)
        grad_c = fetch(table_ref, slice(256, 384), hot_c)
        other, centre = edge_block(spot, geo, grad_c, grad_n)
        ox_ref[8:16] += scatter(other, hot_n)
        yc_ref[0:8] += scatter(centre, hot_c)
        return carry

    lax.fori_loop(1, blocks, lone, 0)


def call(kernel, out_shape, in_specs, out_specs, scratch, cost, limit=VMEM_LIMIT):
    return pl.pallas_call(
        kernel,
        out_shape=out_shape,
        in_specs=in_specs,
        out_specs=out_specs,
        scratch_shapes=scratch,
        compiler_params=pltpu.CompilerParams(vmem_limit_bytes=limit),
        cost_estimate=pl.CostEstimate(flops=cost, bytes_accessed=1 << 20, transcendentals=1 << 18),
    )


def shape(*dims):
    return jax.ShapeDtypeStruct(dims, F32)


IN_VMEM = pl.BlockSpec(memory_space=pltpu.VMEM)
IN_SMEM = pl.BlockSpec(memory_space=pltpu.SMEM)


BOXES_X, BOXES_Y = 32, 16
RUNGS = [(y, half if y % 2 == 0 else 1 - half) for y in range(8) for half in range(2)]
RUNGS = RUNGS[4:] + RUNGS[:4]
AROUND = {(0, 0): 0, (0, 1): 1, (1, 1): 2, (1, 0): 3}


def at_home(p, q):
    return (p % BOXES_X) * BOXES_Y + q % BOXES_Y


def at_work(p, q):
    chip, core = (p % BOXES_X) // 2, p % 2
    z, left = (chip, 0) if chip < 8 else (15 - chip, 1)
    y, right = RUNGS[q % BOXES_Y]
    x = AROUND[(left, right)]
    return (((y // 4) * 8 + z) * 2 + core) * BOXES_Y + (y % 4) * 4 + x


def odd_box():
    gx, gy = lax.axis_index("gx"), lax.axis_index("gy")
    y = (gx // 16) * 4 + gy // 4
    right = (gy % 4 + 1) // 2
    return gx % 2 == 1, (y + right) % 2 == 1


def move(block, source, target, shift):
    pairs = [
        (source(p + shift[0], q + shift[1]), target(p, q)) for p in range(BOXES_X) for q in range(BOXES_Y)
    ]
    return lax.ppermute(block, ("gx", "gy"), pairs)


def trade(block, axis, first):
    pairs = []
    for p in range(BOXES_X):
        for q in range(BOXES_Y):
            away = 1 if (p, q)[axis] % 2 == first else -1
            pairs.append((at_work(p + away * (axis == 0), q + away * (axis == 1)), at_work(p, q)))
    return lax.ppermute(block, ("gx", "gy"), pairs)


def butterfly(xc, oy, odd_p, odd_q):
    far = jnp.where(odd_p, xc, oy)
    near = jnp.where(odd_p, oy, xc)
    near_in = trade(near, 0, 0)
    far_in = trade(far, 0, 1)
    far, near = far + far_in, near + near_in
    even_p = jnp.logical_not(odd_p)
    here = jnp.where(even_p, far, near)
    beside = jnp.where(even_p, near, far)
    up = jnp.concatenate([here[128:256], beside[128:256]], axis=0)
    down = jnp.concatenate([here[0:128], beside[0:128]], axis=0)
    one = jnp.where(odd_q, up, down)
    two = jnp.where(odd_q, down, up)
    return one, two, trade(one, 1, 1), trade(two, 1, 0)


def local(
    positions, species, neighbours, counts, image_z, send_lists, w_basis, w_center, w_neigh, w_env, w_latent, w_tensor, w_out
):
    own = call(
        pack_kernel,
        shape(24, ATOMS),
        [pl.BlockSpec(memory_space=pl.ANY)] * 6,
        IN_VMEM,
        [
            pltpu.VMEM((3, 1, ATOMS), F32),
            pltpu.VMEM((1, 1, ATOMS), jnp.int32),
            pltpu.VMEM((1, 1, ATOMS), jnp.int32),
            pltpu.VMEM((1, 1, 2 * ATOMS), jnp.int32),
            pltpu.VMEM((SLOTS, ATOMS), jnp.int32),
            pltpu.VMEM((SLOTS, ATOMS), jnp.int32),
            pltpu.SemaphoreType.DMA((6,)),
        ],
        1000,
        60 * 1024 * 1024,
    )(
        positions.transpose(0, 2, 1, 3).reshape(3, 1, ATOMS),
        species,
        counts,
        send_lists,
        neighbours.transpose(0, 1, 3, 2).reshape(SLOTS, ATOMS),
        image_z.transpose(0, 1, 3, 2).reshape(SLOTS, ATOMS),
    )
    odd_p, odd_q = odd_box()
    odd = odd_q.astype(jnp.int32).reshape(1)
    own = move(own, at_home, at_work, (0, 0))
    in_x = move(own[0:8], at_work, at_work, (1, 0))
    in_yc = move(jnp.concatenate([own, in_x], axis=0), at_work, at_work, (0, 1))

    wfeat = jnp.concatenate(
        [w_basis, (w_center[0] + w_neigh[0])[None], (w_center[1] - w_center[0])[None], (w_neigh[1] - w_neigh[0])[None],
         jnp.zeros((5, 128), F32)], axis=0
    ).T
    xc, oy, lat, dlat, wl, geo, count = call(
        first_kernel,
        (shape(256, 128), shape(256, 128), shape(128, 2 * EDGES), shape(128, 2 * EDGES), shape(32, 2 * EDGES),
         shape(16, 2 * EDGES), jax.ShapeDtypeStruct((1,), jnp.int32)),
        [IN_VMEM] * 5,
        (IN_VMEM,) * 6 + (IN_SMEM,),
        [pltpu.VMEM((16, ATOMS), F32)],
        500_000_000,
    )(own, in_x, in_yc, wfeat, w_env.T)
    one, two, one_in, two_in = butterfly(xc, oy, odd_p, odd_q)
    wten = w_tensor.reshape(2 * TC, 128)
    wout = w_out[:, None]
    early, first_read = call(
        early_kernel,
        (shape(128, 2 * EDGES), shape(8, 2 * EDGES)),
        [IN_SMEM] + [IN_VMEM] * 3,
        (IN_VMEM,) * 2,
        [],
        200_000_000,
    )(count, lat, w_latent.T, wout)
    xc, oy, gpre, rows = call(
        second_kernel,
        (shape(256, 128), shape(256, 128), shape(128, 2 * EDGES), shape(8, 2 * EDGES)),
        [IN_SMEM] * 2 + [IN_VMEM] * 10,
        (IN_VMEM,) * 4,
        [pltpu.VMEM((256, 512), BF16)],
        1_000_000_000,
    )(count, odd, one, two, one_in, two_in, early, first_read, geo, wten.T, wten, wout)
    glat = call(
        late_kernel,
        shape(128, 2 * EDGES),
        [IN_SMEM] + [IN_VMEM] * 4,
        IN_VMEM,
        [],
        200_000_000,
    )(count, gpre, geo, w_latent, wout)
    one, two, one_in, two_in = butterfly(xc, oy, odd_p, odd_q)
    yc, ox = call(
        third_kernel,
        (shape(16, 128), shape(16, 128)),
        [IN_SMEM] * 2 + [IN_VMEM] * 11,
        (IN_VMEM,) * 2,
        [pltpu.VMEM((256, 512), BF16)],
        500_000_000,
    )(count, odd, one, two, one_in, two_in, dlat, wl, glat, geo, rows, w_env, w_basis)
    ox = ox + move(yc, at_work, at_work, (0, -1))
    total = move(ox[8:16], at_work, at_home, (-1, 0)) + move(ox[0:8], at_work, at_home, (0, 0))
    return (total[0:3][None, None], total[3][None, None])


def solution(mesh):
    part = P("gx", "gy", None)
    wide = P("gx", "gy", None, None)
    return jax.shard_map(
        local,
        mesh=mesh,
        in_specs=(wide, part, wide, part, wide, part) + (P(),) * 7,
        out_specs=(wide, part),
        check_vma=False,
    )
```

```python
import jax
import jax.numpy as jnp
from jax import lax
from jax.experimental import pallas as pl
from jax.experimental.pallas import tpu as pltpu
from jax.sharding import PartitionSpec as P

F32 = jnp.float32
BF16 = jnp.bfloat16
ATOMS = 128
SLOTS = 8
EDGES = ATOMS * SLOTS
LONE = 128
WIDE = EDGES + LONE
TC = 32
VMEM_LIMIT = 24 * 1024 * 1024


def halves(x):
    high = x.astype(BF16)
    return high, (x - high.astype(F32)).astype(BF16)


def dot_nn(a, b):
    return lax.dot_general(a, b, (((1,), (0,)), ((), ())), preferred_element_type=F32)


def dot_nt(a, b):
    return lax.dot_general(a, b, (((1,), (1,)), ((), ())), preferred_element_type=F32)


def product(left, right):
    a, b = halves(left)
    c, d = halves(right)
    return dot_nn(jnp.concatenate([a, a, b], axis=1), jnp.concatenate([c, d, c], axis=0))


def one_hot(index_row, rows):
    lines = lax.broadcasted_iota(jnp.int32, (rows, index_row.shape[1]), 0)
    return jnp.where(lines == index_row, 1.0, 0.0).astype(BF16)


def scatter(values, hot):
    rows = values.shape[0]
    both = dot_nt(jnp.concatenate(halves(values), axis=0), hot)
    return both[0:rows] + both[rows:]


def fold(values):
    return sum(values[:, k * ATOMS : (k + 1) * ATOMS] for k in range(SLOTS))


def lanes(table, index):
    return jnp.take_along_axis(table, index, axis=1, mode="promise_in_bounds")


def spread(row):
    return jnp.broadcast_to(row, (8, row.shape[1]))


def sigmoid_parts(pre):
    gate = 1.0 / (1.0 + jnp.exp(-pre))
    value = pre * gate
    return value, gate + value * (1.0 - gate)


def four(weight, unit, sign):
    parts = [weight]
    for comp in range(3):
        parts.append((sign * weight) * unit[comp])
    return jnp.concatenate(parts, axis=0)


def basis_of(radius):
    step = lax.broadcasted_iota(jnp.int32, (8, radius.shape[1]), 0).astype(F32)
    gap = radius - (0.5 + 2.5 * step / 7.0)
    return jnp.exp(-4.0 * gap * gap), gap


def unit_rows(geo):
    return [geo[0:1], geo[1:2], geo[2:3]]


def geometry(dx, dy, dz, live):
    radius_sq = dx * dx + dy * dy + dz * dz + 0.25
    radius = jnp.sqrt(radius_sq)
    inverse = 1.0 / radius
    envelope = live * jnp.exp(-0.25 * radius_sq)
    return dx * inverse, dy * inverse, dz * inverse, envelope, radius


def pack_kernel(positions, species, counts, sends, neighbours, images, own_ref):
    lists = sends[0].astype(F32)
    rows = [positions[0], positions[1], positions[2], species[0].astype(F32), lists[:, 0:ATOMS], lists[:, ATOMS:]]
    rows += [counts[0].astype(F32), jnp.zeros((1, ATOMS), F32)]
    for line, values in enumerate(rows):
        own_ref[line : line + 1] = values
    own_ref[8:16] = neighbours[...].astype(F32)
    own_ref[16:24] = images[...].astype(F32)


def first_kernel(
    own_ref, x_ref, yc_ref, wfeat_ref, wenv_ref, xc_ref, oy_ref, lat_ref, dlat_ref, wl_ref, geo_ref, count_ref, rank_ref
):
    sub = lax.broadcasted_iota(jnp.int32, (SLOTS, ATOMS), 0)
    lane = lax.broadcasted_iota(jnp.int32, (SLOTS, ATOMS), 1)
    x_send = x_ref[5:6]
    list_low = spread(x_ref[4:5])
    list_high = jnp.where(lane < 64, spread(yc_ref[5:6]), jnp.where(lane < 96, spread(yc_ref[29:30]), spread(x_send)))

    neigh = own_ref[8:16].astype(jnp.int32)
    live = sub < spread(own_ref[6:7]).astype(jnp.int32)
    ghost = neigh - ATOMS
    low = lanes(list_low, jnp.clip(ghost, 0, ATOMS - 1)).astype(jnp.int32)
    high = lanes(list_high, jnp.clip(ghost - ATOMS, 0, ATOMS - 1)).astype(jnp.int32)
    atom = jnp.where(ghost < 0, neigh, jnp.where(ghost < ATOMS, low, high))
    in_x = (ghost >= 0) & (ghost < 128)
    in_y = (ghost >= 128) & (ghost < 192)
    in_c = ghost >= 192
    live = live & (ghost < 224)

    def pick(line):
        values = lanes(spread(own_ref[line : line + 1]), atom)
        values = jnp.where(in_x, lanes(spread(x_ref[line : line + 1]), atom), values)
        values = jnp.where(in_y, lanes(spread(yc_ref[line : line + 1]), atom), values)
        return jnp.where(in_c, lanes(spread(yc_ref[24 + line : 25 + line]), atom), values)

    shift_x = jnp.where(in_x | in_c, 1.0, 0.0)
    shift_y = jnp.where(in_y | in_c, 1.0, 0.0)
    dx = pick(0) + shift_x - own_ref[0:1]
    dy = pick(1) + shift_y - own_ref[1:2]
    dz = pick(2) - own_ref[2:3] + own_ref[16:24]
    rows = list(geometry(dx, dy, dz, jnp.where(live, 1.0, 0.0)))
    rows.append(spread(own_ref[3:4]))
    rows.append(pick(3))
    box = jnp.where(in_x, 128, 0) + jnp.where(in_y, 256, 0) + jnp.where(in_c, 384, 0)
    rows.append((box + atom).astype(F32))
    for line, values in enumerate(rows):
        for k in range(SLOTS):
            geo_ref[line : line + 1, k * ATOMS : (k + 1) * ATOMS] = values[k : k + 1]
    geo_ref[8:16, 0:WIDE] = jnp.zeros((8, WIDE), F32)

    y_neigh = yc_ref[8:16].astype(jnp.int32)
    wanted = (sub < spread(yc_ref[6:7]).astype(jnp.int32)) & (y_neigh >= 352)
    wanted_f = jnp.where(wanted, 1.0, 0.0)
    y_atom = lanes(spread(x_send), jnp.clip(y_neigh - 256, 0, ATOMS - 1))
    before = jnp.where(
        lax.broadcasted_iota(jnp.int32, (ATOMS, ATOMS), 0) <= lax.broadcasted_iota(jnp.int32, (ATOMS, ATOMS), 1), 1.0, 0.0
    ).astype(BF16)
    upto = dot_nn(wanted_f.astype(BF16), before)
    totals = jnp.sum(wanted_f, axis=1, keepdims=True)
    running = jnp.zeros((1, 1), F32)
    starts = []
    for k in range(SLOTS):
        starts.append(running)
        running = running + totals[k : k + 1]
    rank = jnp.where(wanted, upto - 1.0 + jnp.concatenate(starts, axis=0), -1.0)
    rank_ref[0:8] = rank
    rank_ref[8:16] = y_atom
    count = jnp.sum(wanted_f).astype(jnp.int32)
    count_ref[0] = count
    blocks = (count + (LONE - 1)) // LONE

    def compact(block, carry):
        base = (block * LONE).astype(F32)
        line = lax.broadcasted_iota(jnp.int32, (LONE, ATOMS), 0).astype(F32) + base
        packed = jnp.zeros((8, LONE), F32)
        for k in range(SLOTS):
            hot = jnp.where(line == rank_ref[k : k + 1], 1.0, 0.0).astype(BF16)
            feats = jnp.where(sub == 0, lane.astype(F32), 0.0)
            feats = jnp.where(sub == 1, rank_ref[8 + k : 9 + k], feats)
            feats = jnp.where(sub == 2, yc_ref[16 + k : 17 + k], feats)
            feats = jnp.where(sub == 3, 1.0, feats)
            packed = packed + dot_nt(feats.astype(BF16), hot)
        centre = lanes(yc_ref[0:8], spread(packed[0:1]).astype(jnp.int32))
        other = lanes(x_ref[0:8], spread(packed[1:2]).astype(jnp.int32))
        ex = other[0:1] + 1.0 - centre[0:1]
        ey = other[1:2] - 1.0 - centre[1:2]
        ez = other[2:3] - centre[2:3] + packed[2:3]
        found = list(geometry(ex, ey, ez, packed[3:4])) + [centre[3:4], other[3:4], packed[1:2] + 128.0, packed[0:1]]
        spot = pl.ds(pl.multiple_of(EDGES + block * LONE, LONE), LONE)
        for number, values in enumerate(found):
            geo_ref[number : number + 1, spot] = values
        return carry

    compact(jnp.int32(0), 0)
    lax.fori_loop(1, blocks, compact, 0)

    wfeat = wfeat_ref[...]
    wenv = wenv_ref[...]

    def edge_block(spot):
        geo = geo_ref[:, spot]
        basis, _ = basis_of(geo[4:5])
        line = lax.broadcasted_iota(jnp.int32, basis.shape, 0)
        extra = jnp.where(line == 0, 1.0, jnp.where(line == 1, geo[5:6], jnp.where(line == 2, geo[6:7], 0.0)))
        pre = product(wfeat, jnp.concatenate([basis, extra], axis=0))
        latent, slope = sigmoid_parts(pre)
        lat_ref[:, spot] = latent
        dlat_ref[:, spot] = slope
        plain = product(wenv, latent)
        wl_ref[:, spot] = plain
        weight = plain * (0.25 * geo[3:4])
        unit = unit_rows(geo)
        return geo, four(weight, unit, 1.0), four(weight, unit, -1.0)

    spot = pl.ds(0, WIDE)
    geo, centre, other = edge_block(spot)
    sums = scatter(other, one_hot(geo[7:8].astype(jnp.int32), 512))
    oy_ref[0:128] = sums[:, 0:128] + fold(centre)
    xc_ref[0:128] = sums[:, 128:256]
    oy_ref[128:256] = sums[:, 256:384] + scatter(centre[:, EDGES:], one_hot(geo[8:9, EDGES:].astype(jnp.int32), 128))
    xc_ref[128:256] = sums[:, 384:512]

    def lone(block, carry):
        spot = pl.ds(pl.multiple_of(EDGES + block * LONE, LONE), LONE)
        geo, centre, other = edge_block(spot)
        xc_ref[0:128] += scatter(other, one_hot(geo[7:8].astype(jnp.int32) - 128, 128))
        oy_ref[128:256] += scatter(centre, one_hot(geo[8:9].astype(jnp.int32), 128))
        return carry

    lax.fori_loop(1, blocks, lone, 0)


def fill_tables(odd_ref, one_ref, two_ref, one_in_ref, two_in_ref, table_ref):
    odd = odd_ref[0] == 1
    one = one_ref[...] + one_in_ref[...]
    two = two_ref[...] + two_in_ref[...]
    down = jnp.where(odd, two, one)
    up = jnp.where(odd, one, two)
    own = down[0:128]
    for place, values in enumerate((own, down[128:256], up[0:128], up[128:256])):
        high, low = halves(values)
        table_ref[0:128, place * 128 : (place + 1) * 128] = high
        table_ref[128:256, place * 128 : (place + 1) * 128] = low
    return own


def fetch(table_ref, spot, hot):
    both = dot_nn(table_ref[:, spot], hot)
    return both[0:128] + both[128:256]


def project(rows, unit, sign):
    total = rows[0:TC]
    for comp in range(3):
        total = total + (sign * unit[comp]) * rows[(comp + 1) * TC : (comp + 2) * TC]
    return total


def early_kernel(count_ref, lat_ref, wlat_t_ref, wout_ref, pre_ref, read_ref):
    blocks = (count_ref[0] + (LONE - 1)) // LONE
    wout = wout_ref[...]

    def edge_block(spot):
        latent = lat_ref[:, spot]
        pre_ref[:, spot] = product(wlat_t_ref[...], latent)
        read_ref[0:1, spot] = jnp.sum(wout * latent, axis=0, keepdims=True)

    edge_block(pl.ds(0, WIDE))

    def lone(block, carry):
        edge_block(pl.ds(pl.multiple_of(EDGES + block * LONE, LONE), LONE))
        return carry

    lax.fori_loop(1, blocks, lone, 0)


def late_kernel(count_ref, gpre_ref, geo_ref, wlat_ref, wout_ref, glat_ref):
    blocks = (count_ref[0] + (LONE - 1)) // LONE

    def edge_block(spot):
        glat_ref[:, spot] = wout_ref[...] * geo_ref[3:4, spot] + product(wlat_ref[...], gpre_ref[:, spot])

    edge_block(pl.ds(0, WIDE))

    def lone(block, carry):
        edge_block(pl.ds(pl.multiple_of(EDGES + block * LONE, LONE), LONE))
        return carry

    lax.fori_loop(1, blocks, lone, 0)


def second_kernel(
    count_ref, odd_ref, one_ref, two_ref, one_in_ref, two_in_ref, early_ref, first_read_ref, geo_ref, wten_t_ref, wten_ref, wout_ref,
    xc_ref, oy_ref, gpre_ref, rows_ref, table_ref,
):
    own = fill_tables(odd_ref, one_ref, two_ref, one_in_ref, two_in_ref, table_ref)
    blocks = (count_ref[0] + (LONE - 1)) // LONE
    wout = wout_ref[...]

    def edge_block(spot, geo, env_c, env_n):
        unit = unit_rows(geo)
        envelope = geo[3:4]
        both = jnp.concatenate([project(env_c, unit, 1.0), project(env_n, unit, -1.0)], axis=0)
        pre = early_ref[:, spot] + product(wten_t_ref[...], both)
        hidden, slope = sigmoid_parts(pre)
        read = first_read_ref[0:1, spot] + jnp.sum(wout * hidden, axis=0, keepdims=True)
        grad_pre = (wout * envelope) * slope
        gpre_ref[:, spot] = grad_pre
        grad_both = product(wten_ref[...], grad_pre)
        grad_c, grad_n = grad_both[0:TC], grad_both[TC : 2 * TC]
        found = [read, 0.5 * envelope * read]
        for comp in range(3):
            lines = slice((comp + 1) * TC, (comp + 2) * TC)
            found.append(jnp.sum(env_c[lines] * grad_c - env_n[lines] * grad_n, axis=0, keepdims=True))
        for number, values in enumerate(found):
            rows_ref[number : number + 1, spot] = values
        return four(grad_c, unit, 1.0), four(grad_n, unit, -1.0)

    spot = pl.ds(0, WIDE)
    geo = geo_ref[:, spot]
    hot = one_hot(geo[7:8].astype(jnp.int32), 512)
    hot_c = one_hot(geo[8:9, EDGES:].astype(jnp.int32), 128)
    env_n = fetch(table_ref, slice(0, 512), hot)
    env_c = jnp.concatenate([own] * SLOTS + [fetch(table_ref, slice(256, 384), hot_c)], axis=1)
    centre, other = edge_block(spot, geo, env_c, env_n)
    sums = scatter(other, hot)
    oy_ref[0:128] = sums[:, 0:128] + fold(centre)
    xc_ref[0:128] = sums[:, 128:256]
    oy_ref[128:256] = sums[:, 256:384] + scatter(centre[:, EDGES:], hot_c)
    xc_ref[128:256] = sums[:, 384:512]

    def lone(block, carry):
        spot = pl.ds(pl.multiple_of(EDGES + block * LONE, LONE), LONE)
        geo = geo_ref[:, spot]
        hot_n = one_hot(geo[7:8].astype(jnp.int32) - 128, 128)
        hot_c = one_hot(geo[8:9].astype(jnp.int32), 128)
        env_n = fetch(table_ref, slice(128, 256), hot_n)
        env_c = fetch(table_ref, slice(256, 384), hot_c)
        centre, other = edge_block(spot, geo, env_c, env_n)
        xc_ref[0:128] += scatter(other, hot_n)
        oy_ref[128:256] += scatter(centre, hot_c)
        return carry

    lax.fori_loop(1, blocks, lone, 0)


def third_kernel(
    count_ref, odd_ref, one_ref, two_ref, one_in_ref, two_in_ref, dlat_ref, wl_ref, glat_ref, geo_ref, rows_ref, wenv_ref, wbasis_ref,
    yc_ref, ox_ref, table_ref,
):
    own = fill_tables(odd_ref, one_ref, two_ref, one_in_ref, two_in_ref, table_ref)
    blocks = (count_ref[0] + (LONE - 1)) // LONE

    def edge_block(spot, geo, grad_c, grad_n):
        unit = unit_rows(geo)
        envelope, radius = geo[3:4], geo[4:5]
        rows = rows_ref[:, spot]
        plain = wl_ref[:, spot]
        grad_w = 0.25 * (project(grad_c, unit, 1.0) + project(grad_n, unit, -1.0))
        weight = plain * (0.25 * envelope)
        grad_env = rows[0:1] + jnp.sum(grad_w * plain, axis=0, keepdims=True)
        grad_lat = glat_ref[:, spot] + product(wenv_ref[...], grad_w * envelope)
        grad_pre = grad_lat * dlat_ref[:, spot]
        grad_basis = product(wbasis_ref[...], grad_pre)
        basis, gap = basis_of(radius)
        grad_r = jnp.sum(grad_basis * (-8.0 * gap * basis), axis=0, keepdims=True)
        inverse = 1.0 / radius
        along = []
        for comp in range(3):
            lines = slice((comp + 1) * TC, (comp + 2) * TC)
            along.append(rows[2 + comp : 3 + comp] + jnp.sum(weight * (grad_c[lines] - grad_n[lines]), axis=0, keepdims=True))
            grad_r = grad_r - along[comp] * unit[comp] * inverse
        grad_sq = grad_r * (0.5 * inverse) - 0.25 * envelope * grad_env
        force = [-(along[comp] * inverse + 2.0 * radius * unit[comp] * grad_sq) for comp in range(3)]
        line = lax.broadcasted_iota(jnp.int32, (8, envelope.shape[1]), 0)
        packed = jnp.where(line == 3, rows[1:2], 0.0)
        for comp in range(3):
            packed = jnp.where(line == comp, force[comp], packed)
        return packed, jnp.where(line == 3, packed, -packed)

    spot = pl.ds(0, WIDE)
    geo = geo_ref[:, spot]
    hot = one_hot(geo[7:8].astype(jnp.int32), 512)
    hot_c = one_hot(geo[8:9, EDGES:].astype(jnp.int32), 128)
    grad_n = fetch(table_ref, slice(0, 512), hot)
    grad_c = jnp.concatenate([own] * SLOTS + [fetch(table_ref, slice(256, 384), hot_c)], axis=1)
    other, centre = edge_block(spot, geo, grad_c, grad_n)
    sums = scatter(other, hot)
    ox_ref[0:8] = sums[:, 0:128] + fold(centre)
    ox_ref[8:16] = sums[:, 128:256]
    yc_ref[0:8] = sums[:, 256:384] + scatter(centre[:, EDGES:], hot_c)
    yc_ref[8:16] = sums[:, 384:512]

    def lone(block, carry):
        spot = pl.ds(pl.multiple_of(EDGES + block * LONE, LONE), LONE)
        geo = geo_ref[:, spot]
        hot_n = one_hot(geo[7:8].astype(jnp.int32) - 128, 128)
        hot_c = one_hot(geo[8:9].astype(jnp.int32), 128)
        grad_n = fetch(table_ref, slice(128, 256), hot_n)
        grad_c = fetch(table_ref, slice(256, 384), hot_c)
        other, centre = edge_block(spot, geo, grad_c, grad_n)
        ox_ref[8:16] += scatter(other, hot_n)
        yc_ref[0:8] += scatter(centre, hot_c)
        return carry

    lax.fori_loop(1, blocks, lone, 0)


def call(kernel, out_shape, in_specs, out_specs, scratch, cost, limit=VMEM_LIMIT):
    return pl.pallas_call(
        kernel,
        out_shape=out_shape,
        in_specs=in_specs,
        out_specs=out_specs,
        scratch_shapes=scratch,
        compiler_params=pltpu.CompilerParams(vmem_limit_bytes=limit),
        cost_estimate=pl.CostEstimate(flops=cost, bytes_accessed=1 << 20, transcendentals=1 << 18),
    )


def shape(*dims):
    return jax.ShapeDtypeStruct(dims, F32)


IN_VMEM = pl.BlockSpec(memory_space=pltpu.VMEM)
IN_SMEM = pl.BlockSpec(memory_space=pltpu.SMEM)


BOXES_X, BOXES_Y = 32, 16
RUNGS = [(y, half if y % 2 == 0 else 1 - half) for y in range(8) for half in range(2)]
RUNGS = RUNGS[4:] + RUNGS[:4]
AROUND = {(0, 0): 0, (0, 1): 1, (1, 1): 2, (1, 0): 3}


def at_home(p, q):
    return (p % BOXES_X) * BOXES_Y + q % BOXES_Y


def at_work(p, q):
    chip, core = (p % BOXES_X) // 2, p % 2
    z, left = (chip, 0) if chip < 8 else (15 - chip, 1)
    y, right = RUNGS[q % BOXES_Y]
    x = AROUND[(left, right)]
    return (((y // 4) * 8 + z) * 2 + core) * BOXES_Y + (y % 4) * 4 + x


def odd_box():
    gx, gy = lax.axis_index("gx"), lax.axis_index("gy")
    y = (gx // 16) * 4 + gy // 4
    right = (gy % 4 + 1) // 2
    return gx % 2 == 1, (y + right) % 2 == 1


def move(block, source, target, shift):
    pairs = [
        (source(p + shift[0], q + shift[1]), target(p, q)) for p in range(BOXES_X) for q in range(BOXES_Y)
    ]
    return lax.ppermute(block, ("gx", "gy"), pairs)


def trade(block, axis, first):
    pairs = []
    for p in range(BOXES_X):
        for q in range(BOXES_Y):
            away = 1 if (p, q)[axis] % 2 == first else -1
            pairs.append((at_work(p + away * (axis == 0), q + away * (axis == 1)), at_work(p, q)))
    return lax.ppermute(block, ("gx", "gy"), pairs)


def butterfly(xc, oy, odd_p, odd_q):
    far = jnp.where(odd_p, xc, oy)
    near = jnp.where(odd_p, oy, xc)
    near_in = trade(near, 0, 0)
    far_in = trade(far, 0, 1)
    far, near = far + far_in, near + near_in
    even_p = jnp.logical_not(odd_p)
    here = jnp.where(even_p, far, near)
    beside = jnp.where(even_p, near, far)
    up = jnp.concatenate([here[128:256], beside[128:256]], axis=0)
    down = jnp.concatenate([here[0:128], beside[0:128]], axis=0)
    one = jnp.where(odd_q, up, down)
    two = jnp.where(odd_q, down, up)
    return one, two, trade(one, 1, 1), trade(two, 1, 0)


def local(
    positions, species, neighbours, counts, image_z, send_lists, w_basis, w_center, w_neigh, w_env, w_latent, w_tensor, w_out
):
    own = call(
        pack_kernel,
        shape(24, ATOMS),
        [IN_VMEM] * 6,
        IN_VMEM,
        [],
        1000,
        60 * 1024 * 1024,
    )(
        positions.transpose(0, 2, 1, 3).reshape(3, 1, ATOMS),
        species,
        counts,
        send_lists,
        neighbours.transpose(0, 1, 3, 2).reshape(SLOTS, ATOMS),
        image_z.transpose(0, 1, 3, 2).reshape(SLOTS, ATOMS),
    )
    odd_p, odd_q = odd_box()
    odd = odd_q.astype(jnp.int32).reshape(1)
    own = move(own, at_home, at_work, (0, 0))
    in_x = move(own[0:8], at_work, at_work, (1, 0))
    in_yc = move(jnp.concatenate([own, in_x], axis=0), at_work, at_work, (0, 1))

    wfeat = jnp.concatenate(
        [w_basis, (w_center[0] + w_neigh[0])[None], (w_center[1] - w_center[0])[None], (w_neigh[1] - w_neigh[0])[None],
         jnp.zeros((5, 128), F32)], axis=0
    ).T
    xc, oy, lat, dlat, wl, geo, count = call(
        first_kernel,
        (shape(256, 128), shape(256, 128), shape(128, 2 * EDGES), shape(128, 2 * EDGES), shape(32, 2 * EDGES),
         shape(16, 2 * EDGES), jax.ShapeDtypeStruct((1,), jnp.int32)),
        [IN_VMEM] * 5,
        (IN_VMEM,) * 6 + (IN_SMEM,),
        [pltpu.VMEM((16, ATOMS), F32)],
        500_000_000,
    )(own, in_x, in_yc, wfeat, w_env.T)
    one, two, one_in, two_in = butterfly(xc, oy, odd_p, odd_q)
    wten = w_tensor.reshape(2 * TC, 128)
    wout = w_out[:, None]
    early, first_read = call(
        early_kernel,
        (shape(128, 2 * EDGES), shape(8, 2 * EDGES)),
        [IN_SMEM] + [IN_VMEM] * 3,
        (IN_VMEM,) * 2,
        [],
        200_000_000,
    )(count, lat, w_latent.T, wout)
    xc, oy, gpre, rows = call(
        second_kernel,
        (shape(256, 128), shape(256, 128), shape(128, 2 * EDGES), shape(8, 2 * EDGES)),
        [IN_SMEM] * 2 + [IN_VMEM] * 10,
        (IN_VMEM,) * 4,
        [pltpu.VMEM((256, 512), BF16)],
        1_000_000_000,
    )(count, odd, one, two, one_in, two_in, early, first_read, geo, wten.T, wten, wout)
    glat = call(
        late_kernel,
        shape(128, 2 * EDGES),
        [IN_SMEM] + [IN_VMEM] * 4,
        IN_VMEM,
        [],
        200_000_000,
    )(count, gpre, geo, w_latent, wout)
    one, two, one_in, two_in = butterfly(xc, oy, odd_p, odd_q)
    yc, ox = call(
        third_kernel,
        (shape(16, 128), shape(16, 128)),
        [IN_SMEM] * 2 + [IN_VMEM] * 11,
        (IN_VMEM,) * 2,
        [pltpu.VMEM((256, 512), BF16)],
        500_000_000,
    )(count, odd, one, two, one_in, two_in, dlat, wl, glat, geo, rows, w_env, w_basis)
    ox = ox + move(yc, at_work, at_work, (0, -1))
    total = move(ox[8:16], at_work, at_home, (-1, 0)) + move(ox[0:8], at_work, at_home, (0, 0))
    return (total[0:3][None, None], total[3][None, None])


def solution(mesh):
    part = P("gx", "gy", None)
    wide = P("gx", "gy", None, None)
    return jax.shard_map(
        local,
        mesh=mesh,
        in_specs=(wide, part, wide, part, wide, part) + (P(),) * 7,
        out_specs=(wide, part),
        check_vma=False,
    )
```

```python
import jax
import jax.numpy as jnp
from jax import lax
from jax.experimental import pallas as pl
from jax.experimental.pallas import tpu as pltpu
from jax.sharding import PartitionSpec as P

F32 = jnp.float32
BF16 = jnp.bfloat16
ATOMS = 128
SLOTS = 8
EDGES = ATOMS * SLOTS
LONE = 128
WIDE = EDGES + LONE
TC = 32
VMEM_LIMIT = 24 * 1024 * 1024


def halves(x):
    high = x.astype(BF16)
    return high, (x - high.astype(F32)).astype(BF16)


def dot_nn(a, b):
    return lax.dot_general(a, b, (((1,), (0,)), ((), ())), preferred_element_type=F32)


def dot_nt(a, b):
    return lax.dot_general(a, b, (((1,), (1,)), ((), ())), preferred_element_type=F32)


def product(left, right):
    a, b = halves(left)
    c, d = halves(right)
    return dot_nn(jnp.concatenate([a, a, b], axis=1), jnp.concatenate([c, d, c], axis=0))


def one_hot(index_row, rows):
    lines = lax.broadcasted_iota(jnp.int32, (rows, index_row.shape[1]), 0)
    return jnp.where(lines == index_row, 1.0, 0.0).astype(BF16)


def scatter(values, hot):
    rows = values.shape[0]
    both = dot_nt(jnp.concatenate(halves(values), axis=0), hot)
    return both[0:rows] + both[rows:]


def fold(values):
    return sum(values[:, k * ATOMS : (k + 1) * ATOMS] for k in range(SLOTS))


def lanes(table, index):
    return jnp.take_along_axis(table, index, axis=1, mode="promise_in_bounds")


def spread(row):
    return jnp.broadcast_to(row, (8, row.shape[1]))


def sigmoid_parts(pre):
    gate = 1.0 / (1.0 + jnp.exp(-pre))
    value = pre * gate
    return value, gate + value * (1.0 - gate)


def four(weight, unit, sign):
    parts = [weight]
    for comp in range(3):
        parts.append((sign * weight) * unit[comp])
    return jnp.concatenate(parts, axis=0)


def basis_of(radius):
    step = lax.broadcasted_iota(jnp.int32, (8, radius.shape[1]), 0).astype(F32)
    gap = radius - (0.5 + 2.5 * step / 7.0)
    return jnp.exp(-4.0 * gap * gap), gap


def unit_rows(geo):
    return [geo[0:1], geo[1:2], geo[2:3]]


def geometry(dx, dy, dz, live):
    radius_sq = dx * dx + dy * dy + dz * dz + 0.25
    radius = jnp.sqrt(radius_sq)
    inverse = 1.0 / radius
    envelope = live * jnp.exp(-0.25 * radius_sq)
    return dx * inverse, dy * inverse, dz * inverse, envelope, radius


def pack_kernel(positions, species, counts, sends, neighbours, images, own_ref):
    lists = sends[0].astype(F32)
    rows = [positions[0], positions[1], positions[2], species[0].astype(F32), lists[:, 0:ATOMS], lists[:, ATOMS:]]
    rows += [counts[0].astype(F32), jnp.zeros((1, ATOMS), F32)]
    for line, values in enumerate(rows):
        own_ref[line : line + 1] = values
    own_ref[8:16] = neighbours[...].astype(F32)
    own_ref[16:24] = images[...].astype(F32)


def first_kernel(
    own_ref, x_ref, yc_ref, wfeat_ref, wenv_ref, xc_ref, oy_ref, lat_ref, dlat_ref, wl_ref, geo_ref, count_ref, rank_ref
):
    sub = lax.broadcasted_iota(jnp.int32, (SLOTS, ATOMS), 0)
    lane = lax.broadcasted_iota(jnp.int32, (SLOTS, ATOMS), 1)
    x_send = x_ref[5:6]
    list_low = spread(x_ref[4:5])
    list_high = jnp.where(lane < 64, spread(yc_ref[5:6]), jnp.where(lane < 96, spread(yc_ref[29:30]), spread(x_send)))

    neigh = own_ref[8:16].astype(jnp.int32)
    live = sub < spread(own_ref[6:7]).astype(jnp.int32)
    ghost = neigh - ATOMS
    low = lanes(list_low, jnp.clip(ghost, 0, ATOMS - 1)).astype(jnp.int32)
    high = lanes(list_high, jnp.clip(ghost - ATOMS, 0, ATOMS - 1)).astype(jnp.int32)
    atom = jnp.where(ghost < 0, neigh, jnp.where(ghost < ATOMS, low, high))
    in_x = (ghost >= 0) & (ghost < 128)
    in_y = (ghost >= 128) & (ghost < 192)
    in_c = ghost >= 192
    live = live & (ghost < 224)

    def pick(line):
        values = lanes(spread(own_ref[line : line + 1]), atom)
        values = jnp.where(in_x, lanes(spread(x_ref[line : line + 1]), atom), values)
        values = jnp.where(in_y, lanes(spread(yc_ref[line : line + 1]), atom), values)
        return jnp.where(in_c, lanes(spread(yc_ref[24 + line : 25 + line]), atom), values)

    shift_x = jnp.where(in_x | in_c, 1.0, 0.0)
    shift_y = jnp.where(in_y | in_c, 1.0, 0.0)
    dx = pick(0) + shift_x - own_ref[0:1]
    dy = pick(1) + shift_y - own_ref[1:2]
    dz = pick(2) - own_ref[2:3] + own_ref[16:24]
    rows = list(geometry(dx, dy, dz, jnp.where(live, 1.0, 0.0)))
    rows.append(spread(own_ref[3:4]))
    rows.append(pick(3))
    box = jnp.where(in_x, 128, 0) + jnp.where(in_y, 256, 0) + jnp.where(in_c, 384, 0)
    rows.append((box + atom).astype(F32))
    for line, values in enumerate(rows):
        for k in range(SLOTS):
            geo_ref[line : line + 1, k * ATOMS : (k + 1) * ATOMS] = values[k : k + 1]
    geo_ref[8:16, 0:WIDE] = jnp.zeros((8, WIDE), F32)

    y_neigh = yc_ref[8:16].astype(jnp.int32)
    wanted = (sub < spread(yc_ref[6:7]).astype(jnp.int32)) & (y_neigh >= 352)
    wanted_f = jnp.where(wanted, 1.0, 0.0)
    y_atom = lanes(spread(x_send), jnp.clip(y_neigh - 256, 0, ATOMS - 1))
    before = jnp.where(
        lax.broadcasted_iota(jnp.int32, (ATOMS, ATOMS), 0) <= lax.broadcasted_iota(jnp.int32, (ATOMS, ATOMS), 1), 1.0, 0.0
    ).astype(BF16)
    upto = dot_nn(wanted_f.astype(BF16), before)
    totals = jnp.sum(wanted_f, axis=1, keepdims=True)
    running = jnp.zeros((1, 1), F32)
    starts = []
    for k in range(SLOTS):
        starts.append(running)
        running = running + totals[k : k + 1]
    rank = jnp.where(wanted, upto - 1.0 + jnp.concatenate(starts, axis=0), -1.0)
    rank_ref[0:8] = rank
    rank_ref[8:16] = y_atom
    count = jnp.sum(wanted_f).astype(jnp.int32)
    count_ref[0] = count
    blocks = (count + (LONE - 1)) // LONE

    def compact(block, carry):
        base = (block * LONE).astype(F32)
        line = lax.broadcasted_iota(jnp.int32, (LONE, ATOMS), 0).astype(F32) + base
        packed = jnp.zeros((8, LONE), F32)
        for k in range(SLOTS):
            hot = jnp.where(line == rank_ref[k : k + 1], 1.0, 0.0).astype(BF16)
            feats = jnp.where(sub == 0, lane.astype(F32), 0.0)
            feats = jnp.where(sub == 1, rank_ref[8 + k : 9 + k], feats)
            feats = jnp.where(sub == 2, yc_ref[16 + k : 17 + k], feats)
            feats = jnp.where(sub == 3, 1.0, feats)
            packed = packed + dot_nt(feats.astype(BF16), hot)
        centre = lanes(yc_ref[0:8], spread(packed[0:1]).astype(jnp.int32))
        other = lanes(x_ref[0:8], spread(packed[1:2]).astype(jnp.int32))
        ex = other[0:1] + 1.0 - centre[0:1]
        ey = other[1:2] - 1.0 - centre[1:2]
        ez = other[2:3] - centre[2:3] + packed[2:3]
        found = list(geometry(ex, ey, ez, packed[3:4])) + [centre[3:4], other[3:4], packed[1:2] + 128.0, packed[0:1]]
        spot = pl.ds(pl.multiple_of(EDGES + block * LONE, LONE), LONE)
        for number, values in enumerate(found):
            geo_ref[number : number + 1, spot] = values
        return carry

    compact(jnp.int32(0), 0)
    lax.fori_loop(1, blocks, compact, 0)

    wfeat = wfeat_ref[...]
    wenv = wenv_ref[...]

    def edge_block(spot):
        geo = geo_ref[:, spot]
        basis, _ = basis_of(geo[4:5])
        line = lax.broadcasted_iota(jnp.int32, basis.shape, 0)
        extra = jnp.where(line == 0, 1.0, jnp.where(line == 1, geo[5:6], jnp.where(line == 2, geo[6:7], 0.0)))
        pre = product(wfeat, jnp.concatenate([basis, extra], axis=0))
        latent, slope = sigmoid_parts(pre)
        lat_ref[:, spot] = latent
        dlat_ref[:, spot] = slope
        plain = product(wenv, latent)
        wl_ref[:, spot] = plain
        weight = plain * (0.25 * geo[3:4])
        unit = unit_rows(geo)
        return geo, four(weight, unit, 1.0), four(weight, unit, -1.0)

    spot = pl.ds(0, WIDE)
    geo, centre, other = edge_block(spot)
    sums = scatter(other, one_hot(geo[7:8].astype(jnp.int32), 512))
    oy_ref[0:128] = sums[:, 0:128] + fold(centre)
    xc_ref[0:128] = sums[:, 128:256]
    oy_ref[128:256] = sums[:, 256:384] + scatter(centre[:, EDGES:], one_hot(geo[8:9, EDGES:].astype(jnp.int32), 128))
    xc_ref[128:256] = sums[:, 384:512]

    def lone(block, carry):
        spot = pl.ds(pl.multiple_of(EDGES + block * LONE, LONE), LONE)
        geo, centre, other = edge_block(spot)
        xc_ref[0:128] += scatter(other, one_hot(geo[7:8].astype(jnp.int32) - 128, 128))
        oy_ref[128:256] += scatter(centre, one_hot(geo[8:9].astype(jnp.int32), 128))
        return carry

    lax.fori_loop(1, blocks, lone, 0)


def fill_tables(odd_ref, one_ref, two_ref, one_in_ref, two_in_ref, table_ref):
    odd = odd_ref[0] == 1
    one = one_ref[...] + one_in_ref[...]
    two = two_ref[...] + two_in_ref[...]
    down = jnp.where(odd, two, one)
    up = jnp.where(odd, one, two)
    own = down[0:128]
    for place, values in enumerate((own, down[128:256], up[0:128], up[128:256])):
        high, low = halves(values)
        table_ref[0:128, place * 128 : (place + 1) * 128] = high
        table_ref[128:256, place * 128 : (place + 1) * 128] = low
    return own


def fetch(table_ref, spot, hot):
    both = dot_nn(table_ref[:, spot], hot)
    return both[0:128] + both[128:256]


def project(rows, unit, sign):
    total = rows[0:TC]
    for comp in range(3):
        total = total + (sign * unit[comp]) * rows[(comp + 1) * TC : (comp + 2) * TC]
    return total


def early_kernel(count_ref, lat_ref, wlat_t_ref, wout_ref, pre_ref, read_ref):
    blocks = (count_ref[0] + (LONE - 1)) // LONE
    wout = wout_ref[...]

    def edge_block(spot):
        latent = lat_ref[:, spot]
        pre_ref[:, spot] = product(wlat_t_ref[...], latent)
        read_ref[0:1, spot] = jnp.sum(wout * latent, axis=0, keepdims=True)

    edge_block(pl.ds(0, WIDE))

    def lone(block, carry):
        edge_block(pl.ds(pl.multiple_of(EDGES + block * LONE, LONE), LONE))
        return carry

    lax.fori_loop(1, blocks, lone, 0)


def late_kernel(count_ref, gpre_ref, geo_ref, wlat_ref, wout_ref, glat_ref):
    blocks = (count_ref[0] + (LONE - 1)) // LONE

    def edge_block(spot):
        glat_ref[:, spot] = wout_ref[...] * geo_ref[3:4, spot] + product(wlat_ref[...], gpre_ref[:, spot])

    edge_block(pl.ds(0, WIDE))

    def lone(block, carry):
        edge_block(pl.ds(pl.multiple_of(EDGES + block * LONE, LONE), LONE))
        return carry

    lax.fori_loop(1, blocks, lone, 0)


def second_kernel(
    count_ref, odd_ref, one_ref, two_ref, one_in_ref, two_in_ref, early_ref, first_read_ref, geo_ref, wten_t_ref, wten_ref, wout_ref,
    xc_ref, oy_ref, gpre_ref, rows_ref, table_ref,
):
    own = fill_tables(odd_ref, one_ref, two_ref, one_in_ref, two_in_ref, table_ref)
    blocks = (count_ref[0] + (LONE - 1)) // LONE
    wout = wout_ref[...]

    def edge_block(spot, geo, env_c, env_n):
        unit = unit_rows(geo)
        envelope = geo[3:4]
        both = jnp.concatenate([project(env_c, unit, 1.0), project(env_n, unit, -1.0)], axis=0)
        pre = early_ref[:, spot] + product(wten_t_ref[...], both)
        hidden, slope = sigmoid_parts(pre)
        read = first_read_ref[0:1, spot] + jnp.sum(wout * hidden, axis=0, keepdims=True)
        grad_pre = (wout * envelope) * slope
        gpre_ref[:, spot] = grad_pre
        grad_both = product(wten_ref[...], grad_pre)
        grad_c, grad_n = grad_both[0:TC], grad_both[TC : 2 * TC]
        found = [read, 0.5 * envelope * read]
        for comp in range(3):
            lines = slice((comp + 1) * TC, (comp + 2) * TC)
            found.append(jnp.sum(env_c[lines] * grad_c - env_n[lines] * grad_n, axis=0, keepdims=True))
        for number, values in enumerate(found):
            rows_ref[number : number + 1, spot] = values
        return four(grad_c, unit, 1.0), four(grad_n, unit, -1.0)

    spot = pl.ds(0, WIDE)
    geo = geo_ref[:, spot]
    hot = one_hot(geo[7:8].astype(jnp.int32), 512)
    hot_c = one_hot(geo[8:9, EDGES:].astype(jnp.int32), 128)
    env_n = fetch(table_ref, slice(0, 512), hot)
    env_c = jnp.concatenate([own] * SLOTS + [fetch(table_ref, slice(256, 384), hot_c)], axis=1)
    centre, other = edge_block(spot, geo, env_c, env_n)
    sums = scatter(other, hot)
    oy_ref[0:128] = sums[:, 0:128] + fold(centre)
    xc_ref[0:128] = sums[:, 128:256]
    oy_ref[128:256] = sums[:, 256:384] + scatter(centre[:, EDGES:], hot_c)
    xc_ref[128:256] = sums[:, 384:512]

    def lone(block, carry):
        spot = pl.ds(pl.multiple_of(EDGES + block * LONE, LONE), LONE)
        geo = geo_ref[:, spot]
        hot_n = one_hot(geo[7:8].astype(jnp.int32) - 128, 128)
        hot_c = one_hot(geo[8:9].astype(jnp.int32), 128)
        env_n = fetch(table_ref, slice(128, 256), hot_n)
        env_c = fetch(table_ref, slice(256, 384), hot_c)
        centre, other = edge_block(spot, geo, env_c, env_n)
        xc_ref[0:128] += scatter(other, hot_n)
        oy_ref[128:256] += scatter(centre, hot_c)
        return carry

    lax.fori_loop(1, blocks, lone, 0)


def third_kernel(
    count_ref, odd_ref, one_ref, two_ref, one_in_ref, two_in_ref, dlat_ref, wl_ref, glat_ref, geo_ref, rows_ref, wenv_ref, wbasis_ref,
    yc_ref, ox_ref, table_ref,
):
    own = fill_tables(odd_ref, one_ref, two_ref, one_in_ref, two_in_ref, table_ref)
    blocks = (count_ref[0] + (LONE - 1)) // LONE

    def edge_block(spot, geo, grad_c, grad_n):
        unit = unit_rows(geo)
        envelope, radius = geo[3:4], geo[4:5]
        rows = rows_ref[:, spot]
        plain = wl_ref[:, spot]
        grad_w = 0.25 * (project(grad_c, unit, 1.0) + project(grad_n, unit, -1.0))
        weight = plain * (0.25 * envelope)
        grad_env = rows[0:1] + jnp.sum(grad_w * plain, axis=0, keepdims=True)
        grad_lat = glat_ref[:, spot] + product(wenv_ref[...], grad_w * envelope)
        grad_pre = grad_lat * dlat_ref[:, spot]
        grad_basis = product(wbasis_ref[...], grad_pre)
        basis, gap = basis_of(radius)
        grad_r = jnp.sum(grad_basis * (-8.0 * gap * basis), axis=0, keepdims=True)
        inverse = 1.0 / radius
        along = []
        for comp in range(3):
            lines = slice((comp + 1) * TC, (comp + 2) * TC)
            along.append(rows[2 + comp : 3 + comp] + jnp.sum(weight * (grad_c[lines] - grad_n[lines]), axis=0, keepdims=True))
            grad_r = grad_r - along[comp] * unit[comp] * inverse
        grad_sq = grad_r * (0.5 * inverse) - 0.25 * envelope * grad_env
        force = [-(along[comp] * inverse + 2.0 * radius * unit[comp] * grad_sq) for comp in range(3)]
        line = lax.broadcasted_iota(jnp.int32, (8, envelope.shape[1]), 0)
        packed = jnp.where(line == 3, rows[1:2], 0.0)
        for comp in range(3):
            packed = jnp.where(line == comp, force[comp], packed)
        return packed, jnp.where(line == 3, packed, -packed)

    spot = pl.ds(0, WIDE)
    geo = geo_ref[:, spot]
    hot = one_hot(geo[7:8].astype(jnp.int32), 512)
    hot_c = one_hot(geo[8:9, EDGES:].astype(jnp.int32), 128)
    grad_n = fetch(table_ref, slice(0, 512), hot)
    grad_c = jnp.concatenate([own] * SLOTS + [fetch(table_ref, slice(256, 384), hot_c)], axis=1)
    other, centre = edge_block(spot, geo, grad_c, grad_n)
    sums = scatter(other, hot)
    ox_ref[0:8] = sums[:, 0:128] + fold(centre)
    ox_ref[8:16] = sums[:, 128:256]
    yc_ref[0:8] = sums[:, 256:384] + scatter(centre[:, EDGES:], hot_c)
    yc_ref[8:16] = sums[:, 384:512]

    def lone(block, carry):
        spot = pl.ds(pl.multiple_of(EDGES + block * LONE, LONE), LONE)
        geo = geo_ref[:, spot]
        hot_n = one_hot(geo[7:8].astype(jnp.int32) - 128, 128)
        hot_c = one_hot(geo[8:9].astype(jnp.int32), 128)
        grad_n = fetch(table_ref, slice(128, 256), hot_n)
        grad_c = fetch(table_ref, slice(256, 384), hot_c)
        other, centre = edge_block(spot, geo, grad_c, grad_n)
        ox_ref[8:16] += scatter(other, hot_n)
        yc_ref[0:8] += scatter(centre, hot_c)
        return carry

    lax.fori_loop(1, blocks, lone, 0)


def unpack_kernel(one_ref, two_ref, forces_ref, energy_ref, three, single, sems):
    total = one_ref[...] + two_ref[...]
    for comp in range(3):
        three[comp] = total[comp : comp + 1]
    single[0] = total[3:4]
    copies = [
        pltpu.make_async_copy(three, forces_ref, sems.at[0]),
        pltpu.make_async_copy(single, energy_ref, sems.at[1]),
    ]
    for copy in copies:
        copy.start()
    for copy in copies:
        copy.wait()


def call(kernel, out_shape, in_specs, out_specs, scratch, cost, limit=VMEM_LIMIT):
    return pl.pallas_call(
        kernel,
        out_shape=out_shape,
        in_specs=in_specs,
        out_specs=out_specs,
        scratch_shapes=scratch,
        compiler_params=pltpu.CompilerParams(vmem_limit_bytes=limit),
        cost_estimate=pl.CostEstimate(flops=cost, bytes_accessed=1 << 20, transcendentals=1 << 18),
    )


def shape(*dims):
    return jax.ShapeDtypeStruct(dims, F32)


IN_VMEM = pl.BlockSpec(memory_space=pltpu.VMEM)
IN_SMEM = pl.BlockSpec(memory_space=pltpu.SMEM)


BOXES_X, BOXES_Y = 32, 16
RUNGS = [(y, half if y % 2 == 0 else 1 - half) for y in range(8) for half in range(2)]
RUNGS = RUNGS[4:] + RUNGS[:4]
AROUND = {(0, 0): 0, (0, 1): 1, (1, 1): 2, (1, 0): 3}


def at_home(p, q):
    return (p % BOXES_X) * BOXES_Y + q % BOXES_Y


def at_work(p, q):
    chip, core = (p % BOXES_X) // 2, p % 2
    z, left = (chip, 0) if chip < 8 else (15 - chip, 1)
    y, right = RUNGS[q % BOXES_Y]
    x = AROUND[(left, right)]
    return (((y // 4) * 8 + z) * 2 + core) * BOXES_Y + (y % 4) * 4 + x


def odd_box():
    gx, gy = lax.axis_index("gx"), lax.axis_index("gy")
    y = (gx // 16) * 4 + gy // 4
    right = (gy % 4 + 1) // 2
    return gx % 2 == 1, (y + right) % 2 == 1


def move(block, source, target, shift):
    pairs = [
        (source(p + shift[0], q + shift[1]), target(p, q)) for p in range(BOXES_X) for q in range(BOXES_Y)
    ]
    return lax.ppermute(block, ("gx", "gy"), pairs)


def trade(block, axis, first):
    pairs = []
    for p in range(BOXES_X):
        for q in range(BOXES_Y):
            away = 1 if (p, q)[axis] % 2 == first else -1
            pairs.append((at_work(p + away * (axis == 0), q + away * (axis == 1)), at_work(p, q)))
    return lax.ppermute(block, ("gx", "gy"), pairs)


def butterfly(xc, oy, odd_p, odd_q):
    far = jnp.where(odd_p, xc, oy)
    near = jnp.where(odd_p, oy, xc)
    near_in = trade(near, 0, 0)
    far_in = trade(far, 0, 1)
    far, near = far + far_in, near + near_in
    even_p = jnp.logical_not(odd_p)
    here = jnp.where(even_p, far, near)
    beside = jnp.where(even_p, near, far)
    up = jnp.concatenate([here[128:256], beside[128:256]], axis=0)
    down = jnp.concatenate([here[0:128], beside[0:128]], axis=0)
    one = jnp.where(odd_q, up, down)
    two = jnp.where(odd_q, down, up)
    return one, two, trade(one, 1, 1), trade(two, 1, 0)


def local(
    positions, species, neighbours, counts, image_z, send_lists, w_basis, w_center, w_neigh, w_env, w_latent, w_tensor, w_out
):
    own = call(
        pack_kernel,
        shape(24, ATOMS),
        [IN_VMEM] * 6,
        IN_VMEM,
        [],
        1000,
        60 * 1024 * 1024,
    )(
        positions.transpose(0, 2, 1, 3).reshape(3, 1, ATOMS),
        species,
        counts,
        send_lists,
        neighbours.transpose(0, 1, 3, 2).reshape(SLOTS, ATOMS),
        image_z.transpose(0, 1, 3, 2).reshape(SLOTS, ATOMS),
    )
    odd_p, odd_q = odd_box()
    odd = odd_q.astype(jnp.int32).reshape(1)
    own = move(own, at_home, at_work, (0, 0))
    in_x = move(own[0:8], at_work, at_work, (1, 0))
    in_yc = move(jnp.concatenate([own, in_x], axis=0), at_work, at_work, (0, 1))

    wfeat = jnp.concatenate(
        [w_basis, (w_center[0] + w_neigh[0])[None], (w_center[1] - w_center[0])[None], (w_neigh[1] - w_neigh[0])[None],
         jnp.zeros((5, 128), F32)], axis=0
    ).T
    xc, oy, lat, dlat, wl, geo, count = call(
        first_kernel,
        (shape(256, 128), shape(256, 128), shape(128, 2 * EDGES), shape(128, 2 * EDGES), shape(32, 2 * EDGES),
         shape(16, 2 * EDGES), jax.ShapeDtypeStruct((1,), jnp.int32)),
        [IN_VMEM] * 5,
        (IN_VMEM,) * 6 + (IN_SMEM,),
        [pltpu.VMEM((16, ATOMS), F32)],
        500_000_000,
    )(own, in_x, in_yc, wfeat, w_env.T)
    one, two, one_in, two_in = butterfly(xc, oy, odd_p, odd_q)
    wten = w_tensor.reshape(2 * TC, 128)
    wout = w_out[:, None]
    early, first_read = call(
        early_kernel,
        (shape(128, 2 * EDGES), shape(8, 2 * EDGES)),
        [IN_SMEM] + [IN_VMEM] * 3,
        (IN_VMEM,) * 2,
        [],
        200_000_000,
    )(count, lat, w_latent.T, wout)
    xc, oy, gpre, rows = call(
        second_kernel,
        (shape(256, 128), shape(256, 128), shape(128, 2 * EDGES), shape(8, 2 * EDGES)),
        [IN_SMEM] * 2 + [IN_VMEM] * 10,
        (IN_VMEM,) * 4,
        [pltpu.VMEM((256, 512), BF16)],
        1_000_000_000,
    )(count, odd, one, two, one_in, two_in, early, first_read, geo, wten.T, wten, wout)
    glat = call(
        late_kernel,
        shape(128, 2 * EDGES),
        [IN_SMEM] + [IN_VMEM] * 4,
        IN_VMEM,
        [],
        200_000_000,
    )(count, gpre, geo, w_latent, wout)
    one, two, one_in, two_in = butterfly(xc, oy, odd_p, odd_q)
    yc, ox = call(
        third_kernel,
        (shape(16, 128), shape(16, 128)),
        [IN_SMEM] * 2 + [IN_VMEM] * 11,
        (IN_VMEM,) * 2,
        [pltpu.VMEM((256, 512), BF16)],
        500_000_000,
    )(count, odd, one, two, one_in, two_in, dlat, wl, glat, geo, rows, w_env, w_basis)
    ox = ox + move(yc, at_work, at_work, (0, -1))
    from_left = move(ox[8:16], at_work, at_home, (-1, 0))
    kept = move(ox[0:8], at_work, at_home, (0, 0))
    forces, energy = call(
        unpack_kernel,
        (shape(3, 1, ATOMS), shape(1, 1, ATOMS)),
        [IN_VMEM] * 2,
        (pl.BlockSpec(memory_space=pl.ANY),) * 2,
        [pltpu.VMEM((3, 1, ATOMS), F32), pltpu.VMEM((1, 1, ATOMS), F32), pltpu.SemaphoreType.DMA((2,))],
        1000,
    )(from_left, kept)
    return (forces.reshape(1, 3, 1, ATOMS).transpose(0, 2, 1, 3), energy)


def solution(mesh):
    part = P("gx", "gy", None)
    wide = P("gx", "gy", None, None)
    return jax.shard_map(
        local,
        mesh=mesh,
        in_specs=(wide, part, wide, part, wide, part) + (P(),) * 7,
        out_specs=(wide, part),
        check_vma=False,
    )
```
